32 devices in a mesh: seq: 8 (over z, core), tp: 4 (over y, x).
Axes of the slice: x: 2, y: 2, z: 4, core: 2. Of those that a mesh axis runs over, the one named last changes fastest.
Arguments:
- hidden_in: bfloat16 [3072, 3584], P('seq'), may hold values from -48 to 48
- joined_inputs: bfloat16 [3072, 8192], P('seq', 'tp'), may hold values from -64 to 64
- lengths: int32 [4], replicated, may hold values from 1 to 1536, 3072 in all
- o_weight: bfloat16 [4096, 3584], P('tp'), may hold values from -0.09375 to 0.09375
- gate_up: float32 [2, 3584, 7168], P(None, ('seq', 'tp')), may hold values from -0.09375 to 0.09375
- down_weight: bfloat16 [7168, 3584], P('tp'), may hold values from -0.0625 to 0.0625
- next_weight: bfloat16 [3584, 8192], P(None, 'tp'), may hold values from -0.09375 to 0.09375
- post_attn_gain: float32 [3584], replicated, may hold values from 0.1 to 1.9
- pre_ffw_gain: float32 [3584], replicated, may hold values from 0.1 to 1.9
- post_ffw_gain: float32 [3584], replicated, may hold values from 0.1 to 1.9
- next_gain: float32 [3584], replicated, may hold values from 0.1 to 1.9
Outputs:
- next_qkv: bfloat16 [3072, 8192], P('seq', 'tp')
The draws below stay inside these ranges and needn't reach their ends.
Inputs may be any that keep to these rules, and one draw needn't show every extreme that they name: The lengths of 4 prompts laid end to end; they sum to 3072 and the longest is exactly 1536.
All inputs are finite; a program needn't handle non-finite values.
Results may differ from the reference program's by a relative error of at most 0.022.
Values may be sent and summed in bfloat16 or wider, within the bound.
No kernel may reach another device: no remote copies, remote signals or barrier semaphores. Data moves between devices by JAX's collectives and lax.ppermute only.
A program may use at most 192 MiB of HBM per device.

```python
import math
import jax
import jax.numpy as jnp
import numpy as np
from jax import lax

D = 3584
HEADS = 16
KV_HEADS = 8
HEAD_DIM = 256
FFW = 7168
PROMPTS = 4
TOK_DEV = 384
TOKENS = 3072
MOST = 1536
QKV_COLS = 8192


def draw_hidden_in(key, part):
    key_base, key_rows, key_cols = jax.random.split(key, 3)
    base = jnp.clip(jax.random.normal(key_base, (TOKENS, D), jnp.float32), -4.0, 4.0)
    row_scale = jnp.exp(jax.random.uniform(key_rows, (TOKENS, 1), jnp.float32, -1.15, 1.15))
    col_scale = jnp.exp(jax.random.uniform(key_cols, (1, D), jnp.float32, -1.15, 1.15))
    return (base * row_scale * col_scale).astype(jnp.bfloat16)


def draw_joined_inputs(key, part):
    per_group = HEADS // KV_HEADS
    group_cols = (per_group + 2) * HEAD_DIM
    key_base, key_rows = jax.random.split(key, 2)
    base = jnp.clip(jax.random.normal(key_base, (TOKENS, KV_HEADS, group_cols), jnp.float32), -4.0, 4.0)
    row_scale = jnp.exp(jax.random.uniform(key_rows, (TOKENS, 1, 1), jnp.float32, -1.15, 1.15))
    lanes = jnp.arange(group_cols)[None, None, :]
    base = jnp.where(lanes >= (per_group + 1) * HEAD_DIM, base * row_scale, base)
    return base.reshape(TOKENS, KV_HEADS * group_cols).astype(jnp.bfloat16)


def block_scale(rng, shape, shards, low, top_value):
    def one(axis_at, blocks):
        steps = jax.random.uniform(jax.random.fold_in(jax.random.fold_in(rng, 6), axis_at), (blocks,), jnp.float32, low / len(shards), top_value / len(shards))
        return jnp.repeat(jnp.exp(steps), shape[axis_at] // blocks).reshape((-1,) + (1,) * (len(shape) - axis_at - 1))

    loudness = one(*shards[0])
    for cut in shards[1:]:
        loudness = loudness * one(*cut)
    return loudness


def length_profile(count, total, most, skew):
    portions = [(1 << 20) // math.isqrt(rank ** skew) + 1 for rank in range(2, count + 1)]
    rest, counts = total - most - (count - 1), [1] * (count - 1)
    while rest > 0:
        movable = [i for i in range(count - 1) if counts[i] < most]
        pool, left = sum([portions[i] for i in movable]), rest
        for i in movable:
            addition = min(most - counts[i], max(1, left * portions[i] // pool), rest)
            counts[i] = counts[i] + addition
            rest = rest - addition
    return np.array([most] + counts)


def ragged_sizes(stream_key, count, total, limit, skew):
    if count == 2:
        one = jax.random.randint(stream_key, (), max(1, total - limit), min(limit, total - 1) + 1)
        return jnp.stack([one, total - one])
    tallies = jnp.asarray(length_profile(count, total, limit, skew), jnp.int32)
    pairs = (count - 1) // 2
    donor, receiver = tallies[1:1 + 2 * pairs:2], tallies[2:2 + 2 * pairs:2]
    slack = jnp.minimum(donor - 1, limit - receiver)
    moved = jax.random.randint(jax.random.fold_in(stream_key, 1), (pairs,), 0, 1 << 20) % (slack + 1)
    tallies = tallies.at[1:1 + 2 * pairs:2].set(donor - moved).at[2:2 + 2 * pairs:2].set(receiver + moved)
    return tallies[jax.random.permutation(jax.random.fold_in(stream_key, 2), count)]


def gaussian(key, dims, deviation, reach, cuts=(), held_as=jnp.bfloat16):
    values = jax.random.normal(key, dims, jnp.float32) * deviation
    if len(cuts) > 0:
        values = block_scale(key, dims, cuts, -0.22, 0.18) * values
    return jnp.clip(values, min=-reach, max=reach).astype(held_as)


def setup_inputs(seed: int = 0) -> dict:
    seeds = jax.random.split(jax.random.key(seed), 12)
    return {
        "hidden_in": draw_hidden_in(jax.random.fold_in(seeds[11], 71), 0),
        "joined_inputs": draw_joined_inputs(jax.random.fold_in(seeds[11], 71), 0),
        "lengths": ragged_sizes(seeds[2], PROMPTS, TOKENS, MOST, 2).astype(jnp.int32),
        "o_weight": gaussian(seeds[3], (HEADS * HEAD_DIM, D), (HEADS * HEAD_DIM) ** -0.5, 0.09375, ((0, 4),)),
        "gate_up": gaussian(seeds[4], (2, D, FFW), D ** -0.5, 0.09375, ((1, 32),), jnp.float32),
        "down_weight": gaussian(seeds[5], (FFW, D), FFW ** -0.5, 0.0625, ((0, 4),)),
        "next_weight": gaussian(seeds[6], (D, QKV_COLS), D ** -0.5, 0.09375, ((1, 4),)),
        "post_attn_gain": jnp.clip(1.0 + 0.18 * jax.random.normal(seeds[7], (D,), jnp.float32), 0.1, 1.9),
        "pre_ffw_gain": jnp.clip(1.0 + 0.18 * jax.random.normal(seeds[8], (D,), jnp.float32), 0.1, 1.9),
        "post_ffw_gain": jnp.clip(1.0 + 0.18 * jax.random.normal(seeds[9], (D,), jnp.float32), 0.1, 1.9),
        "next_gain": jnp.clip(1.0 + 0.18 * jax.random.normal(seeds[10], (D,), jnp.float32), 0.1, 1.9),
    }


def rms_norm(values, gain):
    meansq = lax.optimization_barrier(jnp.mean(values * values, axis=-1, keepdims=True))
    return values * lax.rsqrt(meansq + 1e-06) * gain.astype(jnp.float32)

def reference(hidden_in, joined_inputs, lengths, o_weight, gate_up, down_weight, next_weight, post_attn_gain, pre_ffw_gain, post_ffw_gain, next_gain):
    per_group = HEADS // KV_HEADS
    group_cols = (per_group + 2) * HEAD_DIM
    grouped = joined_inputs.reshape(TOKENS, KV_HEADS, group_cols)
    queries = grouped[:, :, :per_group * HEAD_DIM].reshape(TOKENS, KV_HEADS, per_group, HEAD_DIM).astype(jnp.float32)
    keys_all = grouped[:, :, per_group * HEAD_DIM:(per_group + 1) * HEAD_DIM].astype(jnp.float32)
    values_all = grouped[:, :, (per_group + 1) * HEAD_DIM:].astype(jnp.float32)
    ends = jnp.cumsum(lengths).astype(jnp.int32)
    places = jnp.arange(TOKENS, dtype=jnp.int32)
    prompt_ids = lax.optimization_barrier(jnp.sum((places[:, None] >= ends[None, :]).astype(jnp.int32), axis=1))

    def attend_block(block_index):
        first_row = (block_index * TOK_DEV).astype(jnp.int32)
        query_block = lax.dynamic_slice_in_dim(queries, first_row, TOK_DEV, 0)
        query_place = first_row + jnp.arange(TOK_DEV, dtype=jnp.int32)
        query_ids = lax.dynamic_slice_in_dim(prompt_ids, first_row, TOK_DEV, 0)
        scores = jnp.einsum('qgrd,kgd->qgrk', query_block, keys_all) * HEAD_DIM ** (-0.5)
        allowed = (query_ids[:, None] == prompt_ids[None, :]) & (places[None, :] <= query_place[:, None])
        allowed = allowed[:, None, None, :]
        scores = jnp.where(allowed, scores, -jnp.inf)
        peak = lax.optimization_barrier(jnp.max(scores, axis=-1, keepdims=True))
        weights = jnp.where(allowed, jnp.exp(scores - peak), 0.0)
        norm_sum = lax.optimization_barrier(jnp.sum(weights, axis=-1))
        rounded = lax.optimization_barrier(weights.astype(jnp.bfloat16)).astype(jnp.float32)
        blended = jnp.einsum('qgrk,kgd->qgrd', rounded, values_all) / norm_sum[..., None]
        return blended.astype(jnp.bfloat16).reshape(TOK_DEV, HEADS * HEAD_DIM)
    attended = lax.map(attend_block, jnp.arange(TOKENS // TOK_DEV, dtype=jnp.int32)).reshape(TOKENS, HEADS * HEAD_DIM)
    projected = jnp.dot(attended, o_weight, preferred_element_type=jnp.float32)
    residual_mid = hidden_in.astype(jnp.float32) + rms_norm(projected, post_attn_gain)
    ffw_in = rms_norm(residual_mid, pre_ffw_gain).astype(jnp.bfloat16)
    server_gate_up = gate_up.astype(jnp.bfloat16)
    gate = jnp.dot(ffw_in, server_gate_up[0], preferred_element_type=jnp.float32)
    up_part = jnp.dot(ffw_in, server_gate_up[1], preferred_element_type=jnp.float32)
    activated = (jax.nn.gelu(gate, approximate=True) * up_part).astype(jnp.bfloat16)
    ffw_out = jnp.dot(activated, down_weight, preferred_element_type=jnp.float32)
    residual_out = residual_mid + rms_norm(ffw_out, post_ffw_gain)
    next_in = rms_norm(residual_out, next_gain).astype(jnp.bfloat16)
    return jnp.dot(next_in, next_weight, preferred_element_type=jnp.float32).astype(jnp.bfloat16)
```

```python
import functools

import jax
import jax.numpy as jnp
from jax import lax
from jax.experimental import pallas as pl
from jax.experimental.pallas import tpu as pltpu
from jax.sharding import PartitionSpec as P

HEADS = 16
KV_HEADS = 8
HEAD_DIM = 256
PER_GROUP = HEADS // KV_HEADS
GROUP_COLS = (PER_GROUP + 2) * HEAD_DIM
MIB = 1 << 20


def rms_norm(values, gain):
    meansq = jnp.mean(values * values, axis=-1, keepdims=True)
    return values * lax.rsqrt(meansq + 1e-06) * gain


def tp_swap(values, bits):
    size = lax.axis_size("tp")
    return lax.ppermute(values, "tp", [(i, i ^ bits) for i in range(size)])


def seq_swap(values, bits):
    size = lax.axis_size("seq")
    return lax.ppermute(values, "seq", [(i, i ^ bits) for i in range(size)])


def seq_up(values):
    size = lax.axis_size("seq")
    return lax.ppermute(values, "seq", [(i, i + 2) for i in range(size - 2)])


def attention_kernel(ends_ref, place_ref, joined_ref, *refs, block_count, prompts, parts):
    kv_refs = refs[:block_count]
    out_ref, peak, total, acc = refs[block_count:]
    rows = joined_ref.shape[0]
    piece = rows // parts
    first = place_ref[1]
    queries = jnp.concatenate(
        [joined_ref[:, r * HEAD_DIM : (r + 1) * HEAD_DIM] for r in range(PER_GROUP)], axis=0
    )
    stacked = PER_GROUP * rows
    at = first + lax.rem(lax.broadcasted_iota(jnp.int32, (stacked, 1), 0), rows)
    start = jnp.zeros_like(at)
    lowest = jnp.int32(0)
    for p in range(prompts):
        end = ends_ref[p]
        start = jnp.where(at >= end, jnp.maximum(start, end), start)
        lowest = jnp.where(first >= end, jnp.maximum(lowest, end), lowest)

    def scores_of(keys, base):
        scores = lax.dot_general(
            queries, keys, (((1,), (1,)), ((), ())), preferred_element_type=jnp.float32
        ) * (HEAD_DIM ** (-0.5))
        places = base + lax.broadcasted_iota(jnp.int32, (1, rows), 1)
        return jnp.where((places >= start) & (places <= at), scores, -1e30)

    own_keys = joined_ref[:, PER_GROUP * HEAD_DIM : (PER_GROUP + 1) * HEAD_DIM]
    own_values = joined_ref[:, (PER_GROUP + 1) * HEAD_DIM :]
    scores = scores_of(own_keys, first)
    top = jnp.max(scores, axis=1, keepdims=True)
    weights = jnp.exp(scores - top)
    peak[...] = jnp.broadcast_to(top, peak.shape)
    total[...] = jnp.broadcast_to(jnp.sum(weights, axis=1, keepdims=True), total.shape)
    acc[...] = jnp.dot(
        weights.astype(jnp.bfloat16), own_values, preferred_element_type=jnp.float32
    )
    for i in range(block_count):
        base = place_ref[2 + i]

        @pl.when((base >= 0) & (base + rows > lowest) & (base < first))
        def _(i=i, base=base):
            scores = scores_of(kv_refs[i][:, :HEAD_DIM], base)
            before = peak[:, :1]
            top = jnp.maximum(before, jnp.max(scores, axis=1, keepdims=True))
            weights = jnp.exp(scores - top)
            shrink = jnp.exp(before - top)
            peak[...] = jnp.broadcast_to(top, peak.shape)
            total[...] = total[...] * shrink + jnp.sum(weights, axis=1, keepdims=True)
            acc[...] = acc[...] * shrink + jnp.dot(
                weights.astype(jnp.bfloat16),
                kv_refs[i][:, HEAD_DIM:],
                preferred_element_type=jnp.float32,
            )

    result = (acc[...] / total[:, :1]).astype(jnp.bfloat16)
    for j in range(parts):
        to = pl.multiple_of((place_ref[0] ^ j) * piece, piece)
        for r in range(PER_GROUP):
            out_ref[pl.ds(to, piece), r * HEAD_DIM : (r + 1) * HEAD_DIM] = result[
                r * rows + j * piece : r * rows + (j + 1) * piece
            ]


def attend(joined, kv_blocks, bases, ends, tp_index, first, parts):
    rows, cols = joined.shape
    groups = cols // GROUP_COLS
    place = jnp.stack([tp_index, first] + bases).astype(jnp.int32)
    count = len(kv_blocks)
    stacked = PER_GROUP * rows
    return pl.pallas_call(
        functools.partial(
            attention_kernel, block_count=count, prompts=ends.shape[0], parts=parts
        ),
        grid_spec=pltpu.PrefetchScalarGridSpec(
            num_scalar_prefetch=2,
            grid=(groups,),
            in_specs=[pl.BlockSpec((rows, GROUP_COLS), lambda g, *_: (0, g))]
            + [pl.BlockSpec((rows, 2 * HEAD_DIM), lambda g, *_: (0, g))] * count,
            out_specs=pl.BlockSpec((rows, PER_GROUP * HEAD_DIM), lambda g, *_: (0, g)),
            scratch_shapes=[
                pltpu.VMEM((stacked, 128), jnp.float32),
                pltpu.VMEM((stacked, 128), jnp.float32),
                pltpu.VMEM((stacked, HEAD_DIM), jnp.float32),
            ],
        ),
        out_shape=jax.ShapeDtypeStruct((rows, groups * PER_GROUP * HEAD_DIM), jnp.bfloat16),
        compiler_params=pltpu.CompilerParams(vmem_limit_bytes=48 * MIB),
        cost_estimate=pl.CostEstimate(
            flops=groups * 4 * stacked * rows * HEAD_DIM * (count + 1),
            bytes_accessed=rows * cols * 2 + count * rows * groups * HEAD_DIM * 4,
            transcendentals=groups * stacked * rows * (count + 1),
        ),
        name="attention",
    )(ends, place, joined, *kv_blocks)


def gate_up_kernel(place_ref, *refs, parts, buffers, subs):
    x_refs, w_refs = refs[:parts], refs[parts : parts + buffers]
    out_ref, x_all, w_all, acc, sems = refs[parts + buffers :]
    piece = x_refs[0].shape[0]
    depth, both = w_all.shape
    hidden = both // 2
    sub_rows = w_refs[0].shape[1]

    def copies(i):
        found = []
        for k in range(subs):
            to = pl.multiple_of(place_ref[1 + i * subs + k], 16)
            found.append(
                pltpu.make_async_copy(
                    w_refs[i].at[k], w_all.at[pl.ds(to, sub_rows)], sems.at[i * subs + k]
                )
            )
        return found

    for i in range(buffers):
        for copy in copies(i):
            copy.start()
    for k in range(parts):
        x_all[k * piece : (k + 1) * piece] = x_refs[k][...]
    half_depth = depth // 2
    tile = 256 if both % 256 == 0 else 128
    for part in range(2):
        for i in range(part * buffers // 2, (part + 1) * buffers // 2):
            for copy in copies(i):
                copy.wait()
        half = place_ref[0] ^ part
        from_row = pl.multiple_of(half * half_depth, 128)

        @pl.loop(0, both // tile)
        def _(j, part=part, from_row=from_row):
            at = pl.ds(pl.multiple_of(j * tile, tile), tile)
            product = jnp.dot(
                x_all[:, pl.ds(from_row, half_depth)],
                w_all[pl.ds(from_row, half_depth), at],
                preferred_element_type=jnp.float32,
            )
            if part == 0:
                acc[:, at] = product
            else:
                acc[:, at] += product

    out_ref[...] = (
        jax.nn.gelu(acc[:, :hidden], approximate=True) * acc[:, hidden:]
    ).astype(jnp.bfloat16)


def gate_up_act(x_pieces, weights, offsets, half):
    parts, buffers = len(x_pieces), len(weights)
    subs = weights[0].shape[0]
    hidden = weights[0].shape[2] // 2
    piece, depth = x_pieces[0].shape
    rows = parts * piece
    place = jnp.stack([half] + offsets).astype(jnp.int32)
    return pl.pallas_call(
        functools.partial(gate_up_kernel, parts=parts, buffers=buffers, subs=subs),
        in_specs=[pl.BlockSpec(memory_space=pltpu.SMEM)]
        + [pl.BlockSpec(memory_space=pltpu.VMEM)] * parts
        + [pl.BlockSpec(memory_space=pl.ANY)] * buffers,
        out_specs=pl.BlockSpec(memory_space=pltpu.VMEM),
        out_shape=jax.ShapeDtypeStruct((rows, hidden), jnp.bfloat16),
        scratch_shapes=[
            pltpu.VMEM((rows, depth), jnp.bfloat16),
            pltpu.VMEM((depth, 2 * hidden), jnp.bfloat16),
            pltpu.VMEM((rows, 2 * hidden), jnp.float32),
            pltpu.SemaphoreType.DMA((buffers * subs,)),
        ],
        compiler_params=pltpu.CompilerParams(vmem_limit_bytes=48 * MIB),
        cost_estimate=pl.CostEstimate(
            flops=4 * rows * depth * hidden,
            bytes_accessed=depth * hidden * 4 + rows * depth * 2,
            transcendentals=rows * hidden,
        ),
        name="gate_up",
    )(place, *x_pieces, *weights)


def gather_weights(gate_up, tp_index, seq_index):
    seq_count, tp_count = lax.axis_size("seq"), lax.axis_size("tp")
    half_count = seq_count // 2
    half = seq_index // half_count
    piece_rows = gate_up.shape[1]
    units = gate_up.shape[2] // tp_count
    hidden = units // 2
    pieces = []
    for k in range(tp_count):
        cut = lax.dynamic_slice(
            gate_up, (0, 0, (tp_index ^ k) * units), (2, piece_rows, units)
        ).astype(jnp.bfloat16)
        pieces.append(tp_swap(cut, k) if k else cut)

    def columns(which):
        cuts = [lax.dynamic_slice_in_dim(p, which * hidden, hidden, 2) for p in pieces]
        cuts = [jnp.concatenate([cut[0], cut[1]], axis=1) for cut in cuts]
        stack = jnp.stack(cuts)
        if piece_rows % 16 == 0:
            return stack
        ordered = [
            lax.dynamic_index_in_dim(stack, tp_index ^ j, 0, keepdims=False)
            for j in range(tp_count)
        ]
        return jnp.concatenate(ordered, axis=0)[None]

    mine, other = columns(half), columns(1 - half)
    found = {0: mine, half_count: seq_swap(other, half_count)}
    bits = 2
    while bits < half_count:
        for key in list(found):
            found[key ^ bits] = seq_swap(found[key], bits)
        bits *= 2
    for key in list(found):
        found[key ^ 1] = seq_swap(found[key], 1)
    keys = sorted(found)
    subs, sub_rows = mine.shape[0], mine.shape[1]
    offsets = []
    for key in keys:
        base = (seq_index ^ key) * (tp_count * piece_rows)
        for k in range(subs):
            offsets.append(base + (tp_index ^ k) * sub_rows if subs > 1 else base)
    return [found[key] for key in keys], offsets, half


def tp_total(partial, parts):
    piece = partial.shape[0] // parts
    total = partial[:piece].astype(jnp.float32)
    for k in range(1, parts):
        total = total + tp_swap(partial[k * piece : (k + 1) * piece], k).astype(jnp.float32)
    return total


def tp_gather(values, parts):
    return [values] + [tp_swap(values, k) for k in range(1, parts)]


def local(
    hidden_in,
    joined_inputs,
    lengths,
    o_weight,
    gate_up,
    down_weight,
    next_weight,
    post_attn_gain,
    pre_ffw_gain,
    post_ffw_gain,
    next_gain,
):
    seq_count, tp_count = lax.axis_size("seq"), lax.axis_size("tp")
    seq_index, tp_index = lax.axis_index("seq"), lax.axis_index("tp")
    rows = hidden_in.shape[0]
    piece = rows // tp_count
    half_count = seq_count // 2
    groups = joined_inputs.shape[1] // GROUP_COLS

    own_kv = jnp.concatenate(
        [
            joined_inputs[:, g * GROUP_COLS + PER_GROUP * HEAD_DIM : (g + 1) * GROUP_COLS]
            for g in range(groups)
        ],
        axis=1,
    )
    chain = [own_kv]
    for _ in range(seq_count // 4):
        chain.append(seq_up(chain[-1]))
    other = [seq_swap(block, 1) for block in chain]
    blocks, bases = [], []
    for j in range(len(chain)):
        if j:
            blocks.append(chain[j])
            bases.append((seq_index - 2 * j) * rows)
        blocks.append(other[j])
        bases.append(((seq_index ^ 1) - 2 * j) * rows)

    weights, offsets, half = gather_weights(gate_up, tp_index, seq_index)

    ends = jnp.cumsum(lengths).astype(jnp.int32)
    attended = attend(
        joined_inputs, blocks, bases, ends, tp_index, seq_index * rows, tp_count
    )
    projected = jnp.dot(attended, o_weight, preferred_element_type=jnp.float32).astype(
        jnp.bfloat16
    )
    hidden_piece = lax.dynamic_slice_in_dim(hidden_in, tp_index * piece, piece, 0)
    residual_mid = hidden_piece.astype(jnp.float32) + rms_norm(
        tp_total(projected, tp_count), post_attn_gain
    )
    ffw_in = rms_norm(residual_mid, pre_ffw_gain).astype(jnp.bfloat16)
    partner_in = seq_swap(ffw_in, half_count)
    own_act = gate_up_act(tp_gather(ffw_in, tp_count), weights, offsets, half)
    partner_act = gate_up_act(tp_gather(partner_in, tp_count), weights, offsets, half)
    returned = seq_swap(partner_act, half_count)
    activated = jnp.where(
        half == 0,
        jnp.concatenate([own_act, returned], axis=1),
        jnp.concatenate([returned, own_act], axis=1),
    )
    ffw_out = jnp.dot(activated, down_weight, preferred_element_type=jnp.float32).astype(
        jnp.bfloat16
    )
    residual_out = residual_mid + rms_norm(tp_total(ffw_out, tp_count), post_ffw_gain)
    next_in = rms_norm(residual_out, next_gain).astype(jnp.bfloat16)
    next_all = jnp.concatenate(tp_gather(next_in, tp_count), axis=0)
    result = jnp.dot(next_all, next_weight, preferred_element_type=jnp.float32).astype(
        jnp.bfloat16
    )
    return jnp.concatenate(
        [
            lax.dynamic_slice_in_dim(result, (tp_index ^ j) * piece, piece, 0)
            for j in range(tp_count)
        ],
        axis=0,
    )


def solution(mesh):
    in_specs = (
        P("seq", None),
        P("seq", "tp"),
        P(),
        P("tp", None),
        P(None, ("seq", "tp"), None),
        P("tp", None),
        P(None, "tp"),
        P(),
        P(),
        P(),
        P(),
    )
    out_specs = P("seq", "tp")
    return jax.shard_map(local, mesh=mesh, in_specs=in_specs, out_specs=out_specs, check_vma=False)
```

```python
import functools

import jax
import jax.numpy as jnp
from jax import lax
from jax.experimental import pallas as pl
from jax.experimental.pallas import tpu as pltpu
from jax.sharding import PartitionSpec as P

HEADS = 16
KV_HEADS = 8
HEAD_DIM = 256
PER_GROUP = HEADS // KV_HEADS
GROUP_COLS = (PER_GROUP + 2) * HEAD_DIM
MIB = 1 << 20
UNIT = 20_000_000_000
CA = 0.1
CM = 0.1
CC = 1.0
CW = 1.0


def span(units):
    return pl.CostEstimate(flops=int(units * UNIT) + 1, bytes_accessed=1000, transcendentals=0)


COST = span(0)


def rms_norm(values, gain):
    meansq = jnp.mean(values * values, axis=-1, keepdims=True)
    return values * lax.rsqrt(meansq + 1e-06) * gain


def tp_swap(values, bits):
    size = lax.axis_size("tp")
    return lax.ppermute(values, "tp", [(i, i ^ bits) for i in range(size)])


def seq_swap(values, bits):
    size = lax.axis_size("seq")
    return lax.ppermute(values, "seq", [(i, i ^ bits) for i in range(size)])


def seq_up(values):
    size = lax.axis_size("seq")
    return lax.ppermute(values, "seq", [(i, i + 2) for i in range(size - 2)])


def after(values, token):
    return lax.optimization_barrier((values, token))[0]


def hint(values):
    return seq_swap(values[:16, :128], 1)


def attention_kernel(ends_ref, place_ref, joined_ref, o_hbm, *refs, blocks, groups, prompts, parts):
    kv_refs = refs[: blocks * groups]
    out_refs = refs[blocks * groups : blocks * groups + parts]
    peak, total, acc, projected, o_ref, sems = refs[blocks * groups + parts :]
    rows = joined_ref.shape[0]
    piece = rows // parts
    head_cols = PER_GROUP * HEAD_DIM
    fetches = []
    for g in range(groups):
        held = pl.ds(g * head_cols, head_cols)
        fetches.append(pltpu.make_async_copy(o_hbm.at[held], o_ref.at[held], sems.at[g]))
        fetches[-1].start()
    first = place_ref[1]
    stacked = PER_GROUP * rows
    at = first + lax.rem(lax.broadcasted_iota(jnp.int32, (stacked, 1), 0), rows)
    start = jnp.zeros_like(at)
    lowest = jnp.int32(0)
    for p in range(prompts):
        end = ends_ref[p]
        start = jnp.where(at >= end, jnp.maximum(start, end), start)
        lowest = jnp.where(first >= end, jnp.maximum(lowest, end), lowest)

    for g in range(groups):
        col = g * GROUP_COLS
        queries = jnp.concatenate(
            [
                joined_ref[:, col + r * HEAD_DIM : col + (r + 1) * HEAD_DIM]
                for r in range(PER_GROUP)
            ],
            axis=0,
        )

        def scores_of(keys, base, queries=queries):
            scores = lax.dot_general(
                queries, keys, (((1,), (1,)), ((), ())), preferred_element_type=jnp.float32
            ) * (HEAD_DIM ** (-0.5))
            places = base + lax.broadcasted_iota(jnp.int32, (1, rows), 1)
            return jnp.where((places >= start) & (places <= at), scores, -1e30)

        own_keys = joined_ref[:, col + head_cols : col + head_cols + HEAD_DIM]
        own_values = joined_ref[:, col + head_cols + HEAD_DIM : col + GROUP_COLS]
        scores = scores_of(own_keys, first)
        top = jnp.max(scores, axis=1, keepdims=True)
        weights = jnp.exp(scores - top)
        peak[...] = jnp.broadcast_to(top, peak.shape)
        total[...] = jnp.broadcast_to(jnp.sum(weights, axis=1, keepdims=True), total.shape)
        acc[...] = jnp.dot(
            weights.astype(jnp.bfloat16), own_values, preferred_element_type=jnp.float32
        )
        for i in range(blocks):
            base = place_ref[2 + i]
            kv_ref = kv_refs[i * groups + g]

            @pl.when((base >= 0) & (base + rows > lowest) & (base < first))
            def _(base=base, kv_ref=kv_ref, scores_of=scores_of):
                scores = scores_of(kv_ref[:, :HEAD_DIM], base)
                before = peak[:, :1]
                top = jnp.maximum(before, jnp.max(scores, axis=1, keepdims=True))
                weights = jnp.exp(scores - top)
                shrink = jnp.exp(before - top)
                peak[...] = jnp.broadcast_to(top, peak.shape)
                total[...] = total[...] * shrink + jnp.sum(weights, axis=1, keepdims=True)
                acc[...] = acc[...] * shrink + jnp.dot(
                    weights.astype(jnp.bfloat16),
                    kv_ref[:, HEAD_DIM:],
                    preferred_element_type=jnp.float32,
                )

        result = (acc[...] / total[:, :1]).astype(jnp.bfloat16)
        attended = jnp.concatenate(
            [result[r * rows : (r + 1) * rows] for r in range(PER_GROUP)], axis=1
        )
        fetches[g].wait()
        tile = 512
        for j in range(o_ref.shape[1] // tile):
            cut = slice(j * tile, (j + 1) * tile)
            product = jnp.dot(
                attended,
                o_ref[g * head_cols : (g + 1) * head_cols, cut],
                preferred_element_type=jnp.float32,
            )
            if g > 0:
                product = product + projected[:, cut]
            projected[:, cut] = product

    for k in range(parts):
        at_row = pl.multiple_of((place_ref[0] ^ k) * piece, piece)
        out_refs[k][...] = projected[pl.ds(at_row, piece)].astype(jnp.bfloat16)


def attend(joined, o_weight, kv_blocks, bases, ends, tp_index, first, parts):
    rows, cols = joined.shape
    width = o_weight.shape[1]
    groups = cols // GROUP_COLS
    place = jnp.stack([tp_index, first] + bases).astype(jnp.int32)
    count = len(kv_blocks)
    stacked = PER_GROUP * rows
    return pl.pallas_call(
        functools.partial(
            attention_kernel, blocks=count, groups=groups, prompts=ends.shape[0], parts=parts
        ),
        in_specs=[pl.BlockSpec(memory_space=pltpu.SMEM)] * 2
        + [pl.BlockSpec(memory_space=pltpu.VMEM), pl.BlockSpec(memory_space=pl.ANY)]
        + [pl.BlockSpec(memory_space=pltpu.VMEM)] * (count * groups),
        out_specs=[pl.BlockSpec(memory_space=pltpu.VMEM)] * parts,
        scratch_shapes=[
            pltpu.VMEM((stacked, 128), jnp.float32),
            pltpu.VMEM((stacked, 128), jnp.float32),
            pltpu.VMEM((stacked, HEAD_DIM), jnp.float32),
            pltpu.VMEM((rows, width), jnp.float32),
            pltpu.VMEM(o_weight.shape, jnp.bfloat16),
            pltpu.SemaphoreType.DMA((groups,)),
        ],
        out_shape=[jax.ShapeDtypeStruct((rows // parts, width), jnp.bfloat16)] * parts,
        compiler_params=pltpu.CompilerParams(vmem_limit_bytes=48 * MIB),
        cost_estimate=span(CA),
        name="attention",
    )(ends, place, joined, o_weight, *[kv for block in kv_blocks for kv in block])


def mid_norm_kernel(place_ref, hidden_ref, post_ref, pre_ref, *refs, parts):
    residual_ref, out_ref, *chunk_refs = refs[parts:]
    total = refs[0][...].astype(jnp.float32)
    for k in range(1, parts):
        total = total + refs[k][...].astype(jnp.float32)
    residual = hidden_ref[...].astype(jnp.float32) + rms_norm(total, post_ref[...])
    residual_ref[...] = residual
    result = rms_norm(residual, pre_ref[...]).astype(jnp.bfloat16)
    out_ref[...] = result
    for c, ref in enumerate(chunk_refs):
        ref[...] = result[c * ref.shape[0] : (c + 1) * ref.shape[0]]


def mid_norm(hidden, post_gain, pre_gain, partials, tp_index, chunks):
    parts = len(partials)
    shape = partials[0].shape
    cut = (shape[0] // chunks, shape[1])
    whole = pl.BlockSpec(shape, lambda i, *_: (0, 0))
    gain = pl.BlockSpec((1, shape[1]), lambda i, *_: (0, 0))
    return pl.pallas_call(
        functools.partial(mid_norm_kernel, parts=parts),
        grid_spec=pltpu.PrefetchScalarGridSpec(
            num_scalar_prefetch=1,
            grid=(1,),
            in_specs=[pl.BlockSpec(shape, lambda i, place: (place[0], 0)), gain, gain]
            + [whole] * parts,
            out_specs=[whole, whole] + [pl.BlockSpec(cut, lambda i, *_: (0, 0))] * chunks,
        ),
        out_shape=[
            jax.ShapeDtypeStruct(shape, jnp.float32),
            jax.ShapeDtypeStruct(shape, jnp.bfloat16),
        ]
        + [jax.ShapeDtypeStruct(cut, jnp.bfloat16)] * chunks,
        compiler_params=pltpu.CompilerParams(vmem_limit_bytes=32 * MIB),
        cost_estimate=span(CM),
        name="mid_norm",
    )(tp_index[None].astype(jnp.int32), hidden, post_gain[None], pre_gain[None], *partials)


def out_norm_kernel(residual_ref, post_ref, next_ref, *refs, parts):
    total = refs[0][...].astype(jnp.float32)
    for k in range(1, parts):
        total = total + refs[k][...].astype(jnp.float32)
    residual = residual_ref[...] + rms_norm(total, post_ref[...])
    refs[parts][...] = rms_norm(residual, next_ref[...]).astype(jnp.bfloat16)


def out_norm(residual, post_gain, next_gain, partials, chunk):
    parts = len(partials)
    shape = partials[0].shape
    whole = pl.BlockSpec(shape, lambda i: (0, 0))
    gain = pl.BlockSpec((1, shape[1]), lambda i: (0, 0))
    return pl.pallas_call(
        functools.partial(out_norm_kernel, parts=parts),
        grid=(1,),
        in_specs=[pl.BlockSpec(shape, lambda i: (chunk, 0)), gain, gain] + [whole] * parts,
        out_specs=whole,
        out_shape=jax.ShapeDtypeStruct(shape, jnp.bfloat16),
        compiler_params=pltpu.CompilerParams(vmem_limit_bytes=32 * MIB),
        cost_estimate=COST,
        name="out_norm",
    )(residual, post_gain[None], next_gain[None], *partials)


def hold_kernel(mark_ref, src_ref, out_ref, sems):
    rows = src_ref.shape[0] // sems.shape[0]
    copies = [
        pltpu.make_async_copy(
            src_ref.at[pl.ds(i * rows, rows)], out_ref.at[pl.ds(i * rows, rows)], sems.at[i]
        )
        for i in range(sems.shape[0])
    ]
    for copy in copies:
        copy.start()
    for copy in copies:
        copy.wait()


def hold(weight, mark):
    return pl.pallas_call(
        hold_kernel,
        in_specs=[pl.BlockSpec(memory_space=pl.ANY)] * 2,
        out_specs=pl.BlockSpec(memory_space=pltpu.VMEM),
        out_shape=jax.ShapeDtypeStruct(weight.shape, weight.dtype),
        scratch_shapes=[pltpu.SemaphoreType.DMA((4,))],
        compiler_params=pltpu.CompilerParams(vmem_limit_bytes=18 * MIB),
        cost_estimate=COST,
        name="hold",
    )(mark, weight)


def down_kernel(half_ref, own_ref, returned_ref, w_ref, *refs, parts, chunk):
    x_all = refs[parts]
    rows, hidden = returned_ref.shape
    piece = rows // parts
    for half in range(2):

        @pl.when(half_ref[0] == half)
        def _(half=half):
            x_all[:, half * hidden : (half + 1) * hidden] = own_ref[chunk * rows : (chunk + 1) * rows]
            x_all[:, (1 - half) * hidden : (2 - half) * hidden] = returned_ref[...]

    tile = 512

    @pl.loop(0, w_ref.shape[1] // tile)
    def _(j):
        at = pl.ds(pl.multiple_of(j * tile, tile), tile)
        product = jnp.dot(x_all[...], w_ref[:, at], preferred_element_type=jnp.float32)
        for k in range(parts):
            refs[k][:, at] = product[k * piece : (k + 1) * piece].astype(jnp.bfloat16)


def down(own, returned, weight, half, parts, chunk):
    rows, hidden = returned.shape
    width = weight.shape[1]
    return pl.pallas_call(
        functools.partial(down_kernel, parts=parts, chunk=chunk),
        in_specs=[pl.BlockSpec(memory_space=pltpu.SMEM)]
        + [pl.BlockSpec(memory_space=pltpu.VMEM)] * 3,
        out_specs=[pl.BlockSpec(memory_space=pltpu.VMEM)] * parts,
        scratch_shapes=[pltpu.VMEM((rows, 2 * hidden), jnp.bfloat16)],
        out_shape=[jax.ShapeDtypeStruct((rows // parts, width), jnp.bfloat16)] * parts,
        compiler_params=pltpu.CompilerParams(vmem_limit_bytes=24 * MIB),
        cost_estimate=COST,
        name="down",
    )(half[None].astype(jnp.int32), own, returned, weight)


def next_kernel(place_ref, *refs, parts, chunk):
    x_refs, w_ref = refs[:parts], refs[parts]
    out_ref, x_all, held, sems = refs[-4:]
    piece = x_refs[0].shape[0]
    for k in range(parts):
        x_all[k * piece : (k + 1) * piece] = x_refs[k][...]
    tile = 512
    copies = []
    for j in range(w_ref.shape[1] // tile):
        at = pl.ds(j * tile, tile)
        product = jnp.dot(x_all[...], w_ref[:, at], preferred_element_type=jnp.float32)
        for k in range(parts):
            held[j, k] = product[k * piece : (k + 1) * piece].astype(jnp.bfloat16)
            to = out_ref.at[place_ref[0] ^ k, chunk, :, at]
            copies.append(pltpu.make_async_copy(held.at[j, k], to, sems.at[j * parts + k]))
            copies[-1].start()
    for copy in copies:
        copy.wait()


def next_projection(pieces, weight, tp_index, chunk, chunks, before):
    parts = len(pieces)
    piece, width = pieces[0].shape
    cols = weight.shape[1]
    tile = 512
    operands = [tp_index[None].astype(jnp.int32), *pieces, weight]
    specs = [pl.BlockSpec(memory_space=pltpu.SMEM)]
    specs += [pl.BlockSpec(memory_space=pltpu.VMEM)] * (parts + 1)
    aliases = {}
    if before is not None:
        aliases = {len(operands): 0}
        operands.append(before)
        specs.append(pl.BlockSpec(memory_space=pl.ANY))
    return pl.pallas_call(
        functools.partial(next_kernel, parts=parts, chunk=chunk),
        in_specs=specs,
        out_specs=pl.BlockSpec(memory_space=pl.ANY),
        scratch_shapes=[
            pltpu.VMEM((parts * piece, width), jnp.bfloat16),
            pltpu.VMEM((cols // tile, parts, piece, tile), jnp.bfloat16),
            pltpu.SemaphoreType.DMA((cols // tile * parts,)),
        ],
        out_shape=jax.ShapeDtypeStruct((parts, chunks, piece, cols), jnp.bfloat16),
        input_output_aliases=aliases,
        compiler_params=pltpu.CompilerParams(vmem_limit_bytes=24 * MIB),
        cost_estimate=COST,
        name="next_projection",
    )(*operands)


def pack_kernel(place_ref, *refs, buffers, marks):
    w_refs, (out_ref, sems) = refs[:buffers], refs[buffers + marks :]
    copies = []
    for ref in w_refs:
        for k in range(ref.shape[0]):
            to = pl.multiple_of(place_ref[len(copies)], 16)
            copies.append(
                pltpu.make_async_copy(
                    ref.at[k], out_ref.at[pl.ds(to, ref.shape[1])], sems.at[len(copies)]
                )
            )
            copies[-1].start()
    for copy in copies:
        copy.wait()


def pack(buffers, offsets, depth, marks):
    wide = buffers[0].shape[2]
    return pl.pallas_call(
        functools.partial(pack_kernel, buffers=len(buffers), marks=len(marks)),
        in_specs=[pl.BlockSpec(memory_space=pltpu.SMEM)]
        + [pl.BlockSpec(memory_space=pl.ANY)] * (len(buffers) + len(marks)),
        out_specs=pl.BlockSpec(memory_space=pltpu.VMEM),
        out_shape=jax.ShapeDtypeStruct((depth, wide), jnp.bfloat16),
        scratch_shapes=[pltpu.SemaphoreType.DMA((len(offsets),))],
        compiler_params=pltpu.CompilerParams(vmem_limit_bytes=16 * MIB),
        cost_estimate=COST,
        name="pack",
    )(jnp.stack(offsets).astype(jnp.int32), *buffers, *marks)


def gate_up_kernel(half_ref, *refs, parts, picked, chunks):
    x_refs, w_refs = refs[:parts], refs[parts : parts + 2]
    out_ref, x_all, acc = refs[parts + 2 :]
    piece = x_refs[0].shape[0] // chunks
    half_depth, both = w_refs[0].shape
    hidden = both // 2
    for i, chunk in enumerate(picked):
        for k in range(parts):
            at = (i * parts + k) * piece
            x_all[at : at + piece] = x_refs[k][chunk * piece : (chunk + 1) * piece]
    tile = 256 if both % 256 == 0 else 128
    near = pl.multiple_of(half_ref[0] * half_depth, 128)
    far = pl.multiple_of((1 - half_ref[0]) * half_depth, 128)

    @pl.loop(0, both // tile)
    def _(j):
        at = pl.ds(pl.multiple_of(j * tile, tile), tile)
        acc[:, at] = jnp.dot(
            x_all[:, pl.ds(near, half_depth)], w_refs[0][:, at], preferred_element_type=jnp.float32
        ) + jnp.dot(
            x_all[:, pl.ds(far, half_depth)], w_refs[1][:, at], preferred_element_type=jnp.float32
        )

    out_ref[...] = (
        jax.nn.gelu(acc[:, :hidden], approximate=True) * acc[:, hidden:]
    ).astype(jnp.bfloat16)


def gate_up_act(pieces, picked, chunks, packed, half):
    parts = len(pieces)
    piece, depth = pieces[0].shape
    rows = parts * piece * len(picked) // chunks
    wide = packed[0].shape[1]
    return pl.pallas_call(
        functools.partial(gate_up_kernel, parts=parts, picked=picked, chunks=chunks),
        in_specs=[pl.BlockSpec(memory_space=pltpu.SMEM)]
        + [pl.BlockSpec(memory_space=pltpu.VMEM)] * (parts + 2),
        out_specs=pl.BlockSpec(memory_space=pltpu.VMEM),
        out_shape=jax.ShapeDtypeStruct((rows, wide // 2), jnp.bfloat16),
        scratch_shapes=[
            pltpu.VMEM((rows, depth), jnp.bfloat16),
            pltpu.VMEM((rows, wide), jnp.float32),
        ],
        compiler_params=pltpu.CompilerParams(vmem_limit_bytes=28 * MIB),
        cost_estimate=COST,
        name="gate_up",
    )(half[None].astype(jnp.int32), *pieces, *packed)


def gather_weights(gate_up, tp_index, seq_index):
    seq_count, tp_count = lax.axis_size("seq"), lax.axis_size("tp")
    half_count = seq_count // 2
    half = seq_index // half_count
    piece_rows = gate_up.shape[1]
    units = gate_up.shape[2] // tp_count
    hidden = units // 2
    pieces = []
    for k in range(tp_count):
        cut = lax.dynamic_slice(
            gate_up, (0, 0, (tp_index ^ k) * units), (2, piece_rows, units)
        ).astype(jnp.bfloat16)
        pieces.append(tp_swap(cut, k) if k else cut)

    def columns(which):
        cuts = [lax.dynamic_slice_in_dim(p, which * hidden, hidden, 2) for p in pieces]
        cuts = [jnp.concatenate([cut[0], cut[1]], axis=1) for cut in cuts]
        stack = jnp.stack(cuts)
        ordered = [
            lax.dynamic_index_in_dim(stack, tp_index ^ j, 0, keepdims=False)
            for j in range(tp_count)
        ]
        return jnp.concatenate(ordered, axis=0)[None]

    if piece_rows % 16 == 0:
        low, high = assemble(pieces)
    else:
        low, high = columns(0), columns(1)
    return low, high


def spread_doubling(low, high, half):
    half_count = lax.axis_size("seq") // 2
    mine, other = jnp.where(half == 0, low, high), jnp.where(half == 0, high, low)
    found = {0: mine, half_count: seq_swap(other, half_count)}
    bits = 2
    while bits < half_count:
        for key in list(found):
            found[key ^ bits] = seq_swap(found[key], bits)
        bits *= 2
    for key in list(found):
        found[key ^ 1] = seq_swap(found[key], 1)
    return found


def spread_line(low, high, half, gates, pack_one):
    chip = lax.axis_index("seq") // 2
    upper = half == 1

    def up(values, first, count):
        pairs = [(s, s + 2) for s in range(2 * first, 2 * (first + count))]
        return lax.ppermute(values, "seq", pairs)

    def down(values, first, count):
        pairs = [(s + 2, s) for s in range(2 * first, 2 * (first + count))]
        return lax.ppermute(values, "seq", pairs)

    low, high = after((low, high), gates[0])
    mine = jnp.where(upper, high, low)
    up_one, down_one = up(high, 0, 3), down(low, 0, 3)
    handed, seen_one = lax.optimization_barrier(((up_one, down_one), gates[1]))
    up_two = up(jnp.where(chip == 0, low, handed[0]), 0, 3)
    down_two = down(jnp.where(chip == 3, high, handed[1]), 0, 3)
    up_two, down_two = after((up_two, down_two), gates[2])
    up_three, down_three = up(up_two, 2, 1), down(down_two, 0, 1)
    inner = (chip == 1) | (chip == 2)
    found = {
        0: mine,
        2: jnp.where(
            inner, jnp.where(upper, down_two, up_two), jnp.where(upper, up_one, down_one)
        ),
        4: jnp.where(upper, up_two, down_two),
    }
    for key in list(found):
        found[key ^ 1] = seq_swap(found[key], 1)
    near = pack_one(found, range(4), [seen_one])
    (up_three, down_three), (near, found[5], _) = lax.optimization_barrier(
        ((up_three, down_three), (near, found[5], gates[3]))
    )
    found[6] = jnp.where(
        inner, jnp.where(upper, up_one, down_one), jnp.where(upper, up_three, down_three)
    )
    found[7] = [seq_swap(found[6][k : k + 1], 1) for k in range(found[6].shape[0])]
    return [near, pack_one(found, range(4, 8), [])]


def pack_half(found, keys, depth, piece_rows, tp_index, seq_index, marks):
    tp_count, half_count = lax.axis_size("tp"), lax.axis_size("seq") // 2
    buffers, offsets = [], []
    for key in keys:
        base = ((seq_index ^ key) % half_count) * (tp_count * piece_rows)
        parts = found[key] if isinstance(found[key], list) else [found[key]]
        subs = sum(part.shape[0] for part in parts)
        sub_rows = parts[0].shape[1]
        buffers += parts
        for k in range(subs):
            offsets.append(base + (tp_index ^ k) * sub_rows if subs > 1 else base)
    return pack(buffers, offsets, depth // 2, marks)


def assemble_kernel(*refs, parts):
    piece_refs, out_refs = refs[:parts], refs[parts:]
    hidden = piece_refs[0].shape[2] // 2
    for k in range(parts):
        for half in range(2):
            for m in range(2):
                out_refs[half][k, :, m * hidden : (m + 1) * hidden] = piece_refs[k][
                    m, :, half * hidden : (half + 1) * hidden
                ]


def assemble(pieces):
    parts = len(pieces)
    _, rows, units = pieces[0].shape
    return pl.pallas_call(
        functools.partial(assemble_kernel, parts=parts),
        out_shape=[jax.ShapeDtypeStruct((parts, rows, units), jnp.bfloat16)] * 2,
        compiler_params=pltpu.CompilerParams(vmem_limit_bytes=32 * MIB),
        cost_estimate=span(CW),
        name="assemble",
    )(*pieces)


def tp_scatter(partials):
    return [tp_swap(part, k) if k else part for k, part in enumerate(partials)]


def tp_gather(values, parts):
    return [values] + [tp_swap(values, k) for k in range(1, parts)]


def local(
    hidden_in,
    joined_inputs,
    lengths,
    o_weight,
    gate_up,
    down_weight,
    next_weight,
    post_attn_gain,
    pre_ffw_gain,
    post_ffw_gain,
    next_gain,
):
    seq_count, tp_count = lax.axis_size("seq"), lax.axis_size("tp")
    seq_index, tp_index = lax.axis_index("seq"), lax.axis_index("tp")
    rows = hidden_in.shape[0]
    half_count = seq_count // 2
    groups = joined_inputs.shape[1] // GROUP_COLS

    own_kv = [
        joined_inputs[:, g * GROUP_COLS + PER_GROUP * HEAD_DIM : (g + 1) * GROUP_COLS]
        for g in range(groups)
    ]
    chain = [own_kv]
    for _ in range(seq_count // 4):
        chain.append([seq_up(kv) for kv in chain[-1]])
    other = [[seq_swap(kv, 1) for kv in block] for block in chain]
    blocks, bases = [], []
    for j in range(len(chain)):
        if j:
            blocks.append(chain[j])
            bases.append((seq_index - 2 * j) * rows)
        blocks.append(other[j])
        bases.append(((seq_index ^ 1) - 2 * j) * rows)

    half = seq_index // half_count
    low, high = gather_weights(after(gate_up, own_kv[0]), tp_index, seq_index)

    ends = jnp.cumsum(lengths).astype(jnp.int32)
    projected = attend(
        joined_inputs, o_weight, blocks, bases, ends, tp_index, seq_index * rows, tp_count
    )
    piece = rows // tp_count
    chunks = 2 if piece % 32 == 0 else 1
    residual_mid, ffw_in, *ffw_in_cuts = mid_norm(
        hidden_in, post_attn_gain, pre_ffw_gain, tp_scatter(projected), tp_index, chunks
    )
    own_pieces = tp_gather(ffw_in, tp_count)
    partner_in = [seq_swap(cut, half_count) for cut in ffw_in_cuts]
    partner_pieces = [tp_gather(cut, tp_count) for cut in partner_in]
    pack_one = lambda found, keys, marks: pack_half(
        found, keys, hidden_in.shape[1], gate_up.shape[1], tp_index, seq_index, marks
    )
    if seq_count == 8:
        gates = [
            chain[-1],
            hint(projected[0]),
            (partner_in[0], own_pieces[:-1]),
            partner_pieces,
        ]
        packed = spread_line(low, high, half, gates, pack_one)
    else:
        found = spread_doubling(low, high, half)
        packed = [pack_one(found, range(at, at + half_count), []) for at in (0, half_count)]
    returned = [
        seq_swap(gate_up_act(pieces, [0], 1, packed, half), half_count)
        for pieces in partner_pieces
    ]
    own_act = gate_up_act(own_pieces, list(range(chunks)), chunks, packed, half)
    down_held = hold(down_weight, partner_pieces[0][0])
    next_held = hold(next_weight, own_act)
    result = None
    gathered = []
    for c in range(chunks):
        ffw_out = down(own_act, returned[c], down_held, half, tp_count, c)
        next_in = out_norm(residual_mid, post_ffw_gain, next_gain, tp_scatter(ffw_out), c)
        gathered.append(tp_gather(next_in, tp_count))
    for c in range(chunks):
        result = next_projection(gathered[c], next_held, tp_index, c, chunks, result)
    return result.reshape(rows, next_weight.shape[1])


def solution(mesh):
    in_specs = (
        P("seq", None),
        P("seq", "tp"),
        P(),
        P("tp", None),
        P(None, ("seq", "tp"), None),
        P("tp", None),
        P(None, "tp"),
        P(),
        P(),
        P(),
        P(),
    )
    out_specs = P("seq", "tp")
    return jax.shard_map(local, mesh=mesh, in_specs=in_specs, out_specs=out_specs, check_vma=False)
```

```python
import functools

import jax
import jax.numpy as jnp
from jax import lax
from jax.experimental import pallas as pl
from jax.experimental.pallas import tpu as pltpu
from jax.sharding import PartitionSpec as P

HEADS = 16
KV_HEADS = 8
HEAD_DIM = 256
PER_GROUP = HEADS // KV_HEADS
GROUP_COLS = (PER_GROUP + 2) * HEAD_DIM
MIB = 1 << 20
UNIT = 20_000_000_000
CA = 0.1
CM = 4.0
CC = 1.0
CW = 1.0


def span(units):
    return pl.CostEstimate(flops=int(units * UNIT) + 1, bytes_accessed=1000, transcendentals=0)


COST = span(0)


def rms_norm(values, gain):
    meansq = jnp.mean(values * values, axis=-1, keepdims=True)
    return values * lax.rsqrt(meansq + 1e-06) * gain


def tp_swap(values, bits):
    size = lax.axis_size("tp")
    return lax.ppermute(values, "tp", [(i, i ^ bits) for i in range(size)])


def seq_swap(values, bits):
    size = lax.axis_size("seq")
    return lax.ppermute(values, "seq", [(i, i ^ bits) for i in range(size)])


def seq_up(values):
    size = lax.axis_size("seq")
    return lax.ppermute(values, "seq", [(i, i + 2) for i in range(size - 2)])


def after(values, token):
    return lax.optimization_barrier((values, token))[0]


def hint(values):
    return seq_swap(values[:16, :128], 1)


def attention_kernel(ends_ref, place_ref, joined_ref, o_hbm, *refs, blocks, groups, prompts, parts):
    kv_refs = refs[: blocks * groups]
    out_refs = refs[blocks * groups : blocks * groups + parts]
    mark_ref, peak, total, acc, projected, o_ref, sems = refs[blocks * groups + parts :]
    rows = joined_ref.shape[0]
    piece = rows // parts
    head_cols = PER_GROUP * HEAD_DIM
    fetches = []
    for g in range(groups):
        held = pl.ds(g * head_cols, head_cols)
        fetches.append(pltpu.make_async_copy(o_hbm.at[held], o_ref.at[held], sems.at[g]))
        fetches[-1].start()
    first = place_ref[1]
    stacked = PER_GROUP * rows
    at = first + lax.rem(lax.broadcasted_iota(jnp.int32, (stacked, 1), 0), rows)
    start = jnp.zeros_like(at)
    lowest = jnp.int32(0)
    for p in range(prompts):
        end = ends_ref[p]
        start = jnp.where(at >= end, jnp.maximum(start, end), start)
        lowest = jnp.where(first >= end, jnp.maximum(lowest, end), lowest)

    for g in range(groups):
        col = g * GROUP_COLS
        queries = jnp.concatenate(
            [
                joined_ref[:, col + r * HEAD_DIM : col + (r + 1) * HEAD_DIM]
                for r in range(PER_GROUP)
            ],
            axis=0,
        )

        def scores_of(keys, base, queries=queries):
            scores = lax.dot_general(
                queries, keys, (((1,), (1,)), ((), ())), preferred_element_type=jnp.float32
            ) * (HEAD_DIM ** (-0.5))
            places = base + lax.broadcasted_iota(jnp.int32, (1, rows), 1)
            return jnp.where((places >= start) & (places <= at), scores, -1e30)

        own_keys = joined_ref[:, col + head_cols : col + head_cols + HEAD_DIM]
        own_values = joined_ref[:, col + head_cols + HEAD_DIM : col + GROUP_COLS]
        scores = scores_of(own_keys, first)
        top = jnp.max(scores, axis=1, keepdims=True)
        weights = jnp.exp(scores - top)
        peak[...] = jnp.broadcast_to(top, peak.shape)
        total[...] = jnp.broadcast_to(jnp.sum(weights, axis=1, keepdims=True), total.shape)
        acc[...] = jnp.dot(
            weights.astype(jnp.bfloat16), own_values, preferred_element_type=jnp.float32
        )
        for i in range(blocks):
            base = place_ref[2 + i]
            kv_ref = kv_refs[i * groups + g]

            @pl.when((base >= 0) & (base + rows > lowest) & (base < first))
            def _(base=base, kv_ref=kv_ref, scores_of=scores_of):
                scores = scores_of(kv_ref[:, :HEAD_DIM], base)
                before = peak[:, :1]
                top = jnp.maximum(before, jnp.max(scores, axis=1, keepdims=True))
                weights = jnp.exp(scores - top)
                shrink = jnp.exp(before - top)
                peak[...] = jnp.broadcast_to(top, peak.shape)
                total[...] = total[...] * shrink + jnp.sum(weights, axis=1, keepdims=True)
                acc[...] = acc[...] * shrink + jnp.dot(
                    weights.astype(jnp.bfloat16),
                    kv_ref[:, HEAD_DIM:],
                    preferred_element_type=jnp.float32,
                )

        result = (acc[...] / total[:, :1]).astype(jnp.bfloat16)
        attended = jnp.concatenate(
            [result[r * rows : (r + 1) * rows] for r in range(PER_GROUP)], axis=1
        )
        fetches[g].wait()
        tile = 512
        for j in range(o_ref.shape[1] // tile):
            cut = slice(j * tile, (j + 1) * tile)
            product = jnp.dot(
                attended,
                o_ref[g * head_cols : (g + 1) * head_cols, cut],
                preferred_element_type=jnp.float32,
            )
            if g > 0:
                product = product + projected[:, cut]
            projected[:, cut] = product

    for k in range(parts):
        at_row = pl.multiple_of((place_ref[0] ^ k) * piece, piece)
        out_refs[k][...] = projected[pl.ds(at_row, piece)].astype(jnp.bfloat16)
    mark_ref[...] = projected[:16, :128].astype(jnp.bfloat16)


def attend(joined, o_weight, kv_blocks, bases, ends, tp_index, first, parts):
    rows, cols = joined.shape
    width = o_weight.shape[1]
    groups = cols // GROUP_COLS
    place = jnp.stack([tp_index, first] + bases).astype(jnp.int32)
    count = len(kv_blocks)
    stacked = PER_GROUP * rows
    return pl.pallas_call(
        functools.partial(
            attention_kernel, blocks=count, groups=groups, prompts=ends.shape[0], parts=parts
        ),
        in_specs=[pl.BlockSpec(memory_space=pltpu.SMEM)] * 2
        + [pl.BlockSpec(memory_space=pltpu.VMEM), pl.BlockSpec(memory_space=pl.ANY)]
        + [pl.BlockSpec(memory_space=pltpu.VMEM)] * (count * groups),
        out_specs=[pl.BlockSpec(memory_space=pltpu.VMEM)] * (parts + 1),
        scratch_shapes=[
            pltpu.VMEM((stacked, 128), jnp.float32),
            pltpu.VMEM((stacked, 128), jnp.float32),
            pltpu.VMEM((stacked, HEAD_DIM), jnp.float32),
            pltpu.VMEM((rows, width), jnp.float32),
            pltpu.VMEM(o_weight.shape, jnp.bfloat16),
            pltpu.SemaphoreType.DMA((groups,)),
        ],
        out_shape=[jax.ShapeDtypeStruct((rows // parts, width), jnp.bfloat16)] * parts
        + [jax.ShapeDtypeStruct((16, 128), jnp.bfloat16)],
        compiler_params=pltpu.CompilerParams(vmem_limit_bytes=48 * MIB),
        cost_estimate=span(CA),
        name="attention",
    )(ends, place, joined, o_weight, *[kv for block in kv_blocks for kv in block])


def mid_norm_kernel(place_ref, hidden_ref, post_ref, pre_ref, *refs, parts):
    residual_ref, out_ref, *chunk_refs = refs[parts:]
    total = refs[0][...].astype(jnp.float32)
    for k in range(1, parts):
        total = total + refs[k][...].astype(jnp.float32)
    residual = hidden_ref[...].astype(jnp.float32) + rms_norm(total, post_ref[...])
    residual_ref[...] = residual
    result = rms_norm(residual, pre_ref[...]).astype(jnp.bfloat16)
    out_ref[...] = result
    for c, ref in enumerate(chunk_refs):
        ref[...] = result[c * ref.shape[0] : (c + 1) * ref.shape[0]]


def mid_norm(hidden, post_gain, pre_gain, partials, tp_index, chunks):
    parts = len(partials)
    shape = partials[0].shape
    cut = (shape[0] // chunks, shape[1])
    whole = pl.BlockSpec(shape, lambda i, *_: (0, 0))
    gain = pl.BlockSpec((1, shape[1]), lambda i, *_: (0, 0))
    return pl.pallas_call(
        functools.partial(mid_norm_kernel, parts=parts),
        grid_spec=pltpu.PrefetchScalarGridSpec(
            num_scalar_prefetch=1,
            grid=(1,),
            in_specs=[pl.BlockSpec(shape, lambda i, place: (place[0], 0)), gain, gain]
            + [whole] * parts,
            out_specs=[whole, whole] + [pl.BlockSpec(cut, lambda i, *_: (0, 0))] * chunks,
        ),
        out_shape=[
            jax.ShapeDtypeStruct(shape, jnp.float32),
            jax.ShapeDtypeStruct(shape, jnp.bfloat16),
        ]
        + [jax.ShapeDtypeStruct(cut, jnp.bfloat16)] * chunks,
        compiler_params=pltpu.CompilerParams(vmem_limit_bytes=32 * MIB),
        cost_estimate=span(CM),
        name="mid_norm",
    )(tp_index[None].astype(jnp.int32), hidden, post_gain[None], pre_gain[None], *partials)


def out_norm_kernel(residual_ref, post_ref, next_ref, *refs, parts):
    total = refs[0][...].astype(jnp.float32)
    for k in range(1, parts):
        total = total + refs[k][...].astype(jnp.float32)
    residual = residual_ref[...] + rms_norm(total, post_ref[...])
    refs[parts][...] = rms_norm(residual, next_ref[...]).astype(jnp.bfloat16)


def out_norm(residual, post_gain, next_gain, partials, chunk):
    parts = len(partials)
    shape = partials[0].shape
    whole = pl.BlockSpec(shape, lambda i: (0, 0))
    gain = pl.BlockSpec((1, shape[1]), lambda i: (0, 0))
    return pl.pallas_call(
        functools.partial(out_norm_kernel, parts=parts),
        grid=(1,),
        in_specs=[pl.BlockSpec(shape, lambda i: (chunk, 0)), gain, gain] + [whole] * parts,
        out_specs=whole,
        out_shape=jax.ShapeDtypeStruct(shape, jnp.bfloat16),
        compiler_params=pltpu.CompilerParams(vmem_limit_bytes=32 * MIB),
        cost_estimate=COST,
        name="out_norm",
    )(residual, post_gain[None], next_gain[None], *partials)


def hold_kernel(mark_ref, src_ref, out_ref, sems):
    rows = src_ref.shape[0] // sems.shape[0]
    copies = [
        pltpu.make_async_copy(
            src_ref.at[pl.ds(i * rows, rows)], out_ref.at[pl.ds(i * rows, rows)], sems.at[i]
        )
        for i in range(sems.shape[0])
    ]
    for copy in copies:
        copy.start()
    for copy in copies:
        copy.wait()


def hold(weight, mark):
    return pl.pallas_call(
        hold_kernel,
        in_specs=[pl.BlockSpec(memory_space=pl.ANY)] * 2,
        out_specs=pl.BlockSpec(memory_space=pltpu.VMEM),
        out_shape=jax.ShapeDtypeStruct(weight.shape, weight.dtype),
        scratch_shapes=[pltpu.SemaphoreType.DMA((4,))],
        compiler_params=pltpu.CompilerParams(vmem_limit_bytes=18 * MIB),
        cost_estimate=COST,
        name="hold",
    )(mark, weight)


def down_kernel(half_ref, own_ref, returned_ref, w_ref, *refs, parts, chunk):
    x_all = refs[parts]
    rows, hidden = returned_ref.shape
    piece = rows // parts
    for half in range(2):

        @pl.when(half_ref[0] == half)
        def _(half=half):
            x_all[:, half * hidden : (half + 1) * hidden] = own_ref[chunk * rows : (chunk + 1) * rows]
            x_all[:, (1 - half) * hidden : (2 - half) * hidden] = returned_ref[...]

    tile = 512

    @pl.loop(0, w_ref.shape[1] // tile)
    def _(j):
        at = pl.ds(pl.multiple_of(j * tile, tile), tile)
        product = jnp.dot(x_all[...], w_ref[:, at], preferred_element_type=jnp.float32)
        for k in range(parts):
            refs[k][:, at] = product[k * piece : (k + 1) * piece].astype(jnp.bfloat16)


def down(own, returned, weight, half, parts, chunk):
    rows, hidden = returned.shape
    width = weight.shape[1]
    return pl.pallas_call(
        functools.partial(down_kernel, parts=parts, chunk=chunk),
        in_specs=[pl.BlockSpec(memory_space=pltpu.SMEM)]
        + [pl.BlockSpec(memory_space=pltpu.VMEM)] * 3,
        out_specs=[pl.BlockSpec(memory_space=pltpu.VMEM)] * parts,
        scratch_shapes=[pltpu.VMEM((rows, 2 * hidden), jnp.bfloat16)],
        out_shape=[jax.ShapeDtypeStruct((rows // parts, width), jnp.bfloat16)] * parts,
        compiler_params=pltpu.CompilerParams(vmem_limit_bytes=24 * MIB),
        cost_estimate=COST,
        name="down",
    )(half[None].astype(jnp.int32), own, returned, weight)


def next_kernel(place_ref, *refs, parts, chunk):
    x_refs, w_ref = refs[:parts], refs[parts]
    out_ref, x_all, held, sems = refs[-4:]
    piece = x_refs[0].shape[0]
    for k in range(parts):
        x_all[k * piece : (k + 1) * piece] = x_refs[k][...]
    tile = 512
    copies = []
    for j in range(w_ref.shape[1] // tile):
        at = pl.ds(j * tile, tile)
        product = jnp.dot(x_all[...], w_ref[:, at], preferred_element_type=jnp.float32)
        for k in range(parts):
            held[j, k] = product[k * piece : (k + 1) * piece].astype(jnp.bfloat16)
            to = out_ref.at[place_ref[0] ^ k, chunk, :, at]
            copies.append(pltpu.make_async_copy(held.at[j, k], to, sems.at[j * parts + k]))
            copies[-1].start()
    for copy in copies:
        copy.wait()


def next_projection(pieces, weight, tp_index, chunk, chunks, before):
    parts = len(pieces)
    piece, width = pieces[0].shape
    cols = weight.shape[1]
    tile = 512
    operands = [tp_index[None].astype(jnp.int32), *pieces, weight]
    specs = [pl.BlockSpec(memory_space=pltpu.SMEM)]
    specs += [pl.BlockSpec(memory_space=pltpu.VMEM)] * (parts + 1)
    aliases = {}
    if before is not None:
        aliases = {len(operands): 0}
        operands.append(before)
        specs.append(pl.BlockSpec(memory_space=pl.ANY))
    return pl.pallas_call(
        functools.partial(next_kernel, parts=parts, chunk=chunk),
        in_specs=specs,
        out_specs=pl.BlockSpec(memory_space=pl.ANY),
        scratch_shapes=[
            pltpu.VMEM((parts * piece, width), jnp.bfloat16),
            pltpu.VMEM((cols // tile, parts, piece, tile), jnp.bfloat16),
            pltpu.SemaphoreType.DMA((cols // tile * parts,)),
        ],
        out_shape=jax.ShapeDtypeStruct((parts, chunks, piece, cols), jnp.bfloat16),
        input_output_aliases=aliases,
        compiler_params=pltpu.CompilerParams(vmem_limit_bytes=24 * MIB),
        cost_estimate=COST,
        name="next_projection",
    )(*operands)


def pack_kernel(place_ref, *refs, buffers, marks):
    w_refs, (out_ref, sems) = refs[:buffers], refs[buffers + marks :]
    copies = []
    for ref in w_refs:
        for k in range(ref.shape[0]):
            to = pl.multiple_of(place_ref[len(copies)], 16)
            copies.append(
                pltpu.make_async_copy(
                    ref.at[k], out_ref.at[pl.ds(to, ref.shape[1])], sems.at[len(copies)]
                )
            )
            copies[-1].start()
    for copy in copies:
        copy.wait()


def pack(buffers, offsets, depth, marks):
    wide = buffers[0].shape[2]
    return pl.pallas_call(
        functools.partial(pack_kernel, buffers=len(buffers), marks=len(marks)),
        in_specs=[pl.BlockSpec(memory_space=pltpu.SMEM)]
        + [pl.BlockSpec(memory_space=pl.ANY)] * (len(buffers) + len(marks)),
        out_specs=pl.BlockSpec(memory_space=pltpu.VMEM),
        out_shape=jax.ShapeDtypeStruct((depth, wide), jnp.bfloat16),
        scratch_shapes=[pltpu.SemaphoreType.DMA((len(offsets),))],
        compiler_params=pltpu.CompilerParams(vmem_limit_bytes=16 * MIB),
        cost_estimate=COST,
        name="pack",
    )(jnp.stack(offsets).astype(jnp.int32), *buffers, *marks)


def gate_up_kernel(half_ref, *refs, parts, picked, chunks):
    x_refs, w_refs = refs[:parts], refs[parts : parts + 2]
    out_ref, x_all, acc = refs[parts + 2 :]
    piece = x_refs[0].shape[0] // chunks
    half_depth, both = w_refs[0].shape
    hidden = both // 2
    for i, chunk in enumerate(picked):
        for k in range(parts):
            at = (i * parts + k) * piece
            x_all[at : at + piece] = x_refs[k][chunk * piece : (chunk + 1) * piece]
    tile = 256 if both % 256 == 0 else 128
    near = pl.multiple_of(half_ref[0] * half_depth, 128)
    far = pl.multiple_of((1 - half_ref[0]) * half_depth, 128)

    @pl.loop(0, both // tile)
    def _(j):
        at = pl.ds(pl.multiple_of(j * tile, tile), tile)
        acc[:, at] = jnp.dot(
            x_all[:, pl.ds(near, half_depth)], w_refs[0][:, at], preferred_element_type=jnp.float32
        ) + jnp.dot(
            x_all[:, pl.ds(far, half_depth)], w_refs[1][:, at], preferred_element_type=jnp.float32
        )

    out_ref[...] = (
        jax.nn.gelu(acc[:, :hidden], approximate=True) * acc[:, hidden:]
    ).astype(jnp.bfloat16)


def gate_up_act(pieces, picked, chunks, packed, half):
    parts = len(pieces)
    piece, depth = pieces[0].shape
    rows = parts * piece * len(picked) // chunks
    wide = packed[0].shape[1]
    return pl.pallas_call(
        functools.partial(gate_up_kernel, parts=parts, picked=picked, chunks=chunks),
        in_specs=[pl.BlockSpec(memory_space=pltpu.SMEM)]
        + [pl.BlockSpec(memory_space=pltpu.VMEM)] * (parts + 2),
        out_specs=pl.BlockSpec(memory_space=pltpu.VMEM),
        out_shape=jax.ShapeDtypeStruct((rows, wide // 2), jnp.bfloat16),
        scratch_shapes=[
            pltpu.VMEM((rows, depth), jnp.bfloat16),
            pltpu.VMEM((rows, wide), jnp.float32),
        ],
        compiler_params=pltpu.CompilerParams(vmem_limit_bytes=28 * MIB),
        cost_estimate=COST,
        name="gate_up",
    )(half[None].astype(jnp.int32), *pieces, *packed)


def gather_weights(gate_up, tp_index, seq_index):
    seq_count, tp_count = lax.axis_size("seq"), lax.axis_size("tp")
    half_count = seq_count // 2
    half = seq_index // half_count
    piece_rows = gate_up.shape[1]
    units = gate_up.shape[2] // tp_count
    hidden = units // 2
    pieces = []
    for k in range(tp_count):
        cut = lax.dynamic_slice(
            gate_up, (0, 0, (tp_index ^ k) * units), (2, piece_rows, units)
        ).astype(jnp.bfloat16)
        pieces.append(tp_swap(cut, k) if k else cut)

    def columns(which):
        cuts = [lax.dynamic_slice_in_dim(p, which * hidden, hidden, 2) for p in pieces]
        cuts = [jnp.concatenate([cut[0], cut[1]], axis=1) for cut in cuts]
        stack = jnp.stack(cuts)
        ordered = [
            lax.dynamic_index_in_dim(stack, tp_index ^ j, 0, keepdims=False)
            for j in range(tp_count)
        ]
        return jnp.concatenate(ordered, axis=0)[None]

    if piece_rows % 16 == 0:
        low, high = assemble(pieces)
    else:
        low, high = columns(0), columns(1)
    return low, high


def spread_doubling(low, high, half):
    half_count = lax.axis_size("seq") // 2
    mine, other = jnp.where(half == 0, low, high), jnp.where(half == 0, high, low)
    found = {0: mine, half_count: seq_swap(other, half_count)}
    bits = 2
    while bits < half_count:
        for key in list(found):
            found[key ^ bits] = seq_swap(found[key], bits)
        bits *= 2
    for key in list(found):
        found[key ^ 1] = seq_swap(found[key], 1)
    return found


def spread_line(low, high, half, gates, pack_one):
    chip = lax.axis_index("seq") // 2
    upper = half == 1

    def up(values, first, count):
        pairs = [(s, s + 2) for s in range(2 * first, 2 * (first + count))]
        return lax.ppermute(values, "seq", pairs)

    def down(values, first, count):
        pairs = [(s + 2, s) for s in range(2 * first, 2 * (first + count))]
        return lax.ppermute(values, "seq", pairs)

    low, high = after((low, high), gates[0])
    mine = jnp.where(upper, high, low)
    up_one, down_one = up(high, 0, 3), down(low, 0, 3)
    handed, seen_one = lax.optimization_barrier(((up_one, down_one), gates[1]))
    up_two = up(jnp.where(chip == 0, low, handed[0]), 0, 3)
    down_two = down(jnp.where(chip == 3, high, handed[1]), 0, 3)
    up_two, down_two = after((up_two, down_two), gates[2])
    up_three, down_three = up(up_two, 2, 1), down(down_two, 0, 1)
    inner = (chip == 1) | (chip == 2)
    found = {
        0: mine,
        2: jnp.where(
            inner, jnp.where(upper, down_two, up_two), jnp.where(upper, up_one, down_one)
        ),
        4: jnp.where(upper, up_two, down_two),
    }
    for key in list(found):
        found[key ^ 1] = seq_swap(found[key], 1)
    near = pack_one(found, range(4), [seen_one])
    (up_three, down_three), (near, found[5], _) = lax.optimization_barrier(
        ((up_three, down_three), (near, found[5], gates[3]))
    )
    found[6] = jnp.where(
        inner, jnp.where(upper, up_one, down_one), jnp.where(upper, up_three, down_three)
    )
    found[7] = [seq_swap(found[6][k : k + 1], 1) for k in range(found[6].shape[0])]
    return [near, pack_one(found, range(4, 8), [])]


def pack_half(found, keys, depth, piece_rows, tp_index, seq_index, marks):
    tp_count, half_count = lax.axis_size("tp"), lax.axis_size("seq") // 2
    buffers, offsets = [], []
    for key in keys:
        base = ((seq_index ^ key) % half_count) * (tp_count * piece_rows)
        parts = found[key] if isinstance(found[key], list) else [found[key]]
        subs = sum(part.shape[0] for part in parts)
        sub_rows = parts[0].shape[1]
        buffers += parts
        for k in range(subs):
            offsets.append(base + (tp_index ^ k) * sub_rows if subs > 1 else base)
    return pack(buffers, offsets, depth // 2, marks)


def assemble_kernel(*refs, parts):
    piece_refs, out_refs = refs[:parts], refs[parts:]
    hidden = piece_refs[0].shape[2] // 2
    for k in range(parts):
        for half in range(2):
            for m in range(2):
                out_refs[half][k, :, m * hidden : (m + 1) * hidden] = piece_refs[k][
                    m, :, half * hidden : (half + 1) * hidden
                ]


def assemble(pieces):
    parts = len(pieces)
    _, rows, units = pieces[0].shape
    return pl.pallas_call(
        functools.partial(assemble_kernel, parts=parts),
        out_shape=[jax.ShapeDtypeStruct((parts, rows, units), jnp.bfloat16)] * 2,
        compiler_params=pltpu.CompilerParams(vmem_limit_bytes=32 * MIB),
        cost_estimate=span(CW),
        name="assemble",
    )(*pieces)


def tp_scatter(partials):
    return [tp_swap(part, k) if k else part for k, part in enumerate(partials)]


def tp_gather(values, parts):
    return [values] + [tp_swap(values, k) for k in range(1, parts)]


def local(
    hidden_in,
    joined_inputs,
    lengths,
    o_weight,
    gate_up,
    down_weight,
    next_weight,
    post_attn_gain,
    pre_ffw_gain,
    post_ffw_gain,
    next_gain,
):
    seq_count, tp_count = lax.axis_size("seq"), lax.axis_size("tp")
    seq_index, tp_index = lax.axis_index("seq"), lax.axis_index("tp")
    rows = hidden_in.shape[0]
    half_count = seq_count // 2
    groups = joined_inputs.shape[1] // GROUP_COLS

    own_kv = [
        joined_inputs[:, g * GROUP_COLS + PER_GROUP * HEAD_DIM : (g + 1) * GROUP_COLS]
        for g in range(groups)
    ]
    chain = [own_kv]
    for _ in range(seq_count // 4):
        chain.append([seq_up(kv) for kv in chain[-1]])
    other = [[seq_swap(kv, 1) for kv in block] for block in chain]
    blocks, bases = [], []
    for j in range(len(chain)):
        if j:
            blocks.append(chain[j])
            bases.append((seq_index - 2 * j) * rows)
        blocks.append(other[j])
        bases.append(((seq_index ^ 1) - 2 * j) * rows)

    half = seq_index // half_count
    low, high = gather_weights(after(gate_up, own_kv[0]), tp_index, seq_index)

    ends = jnp.cumsum(lengths).astype(jnp.int32)
    *projected, mark = attend(
        joined_inputs, o_weight, blocks, bases, ends, tp_index, seq_index * rows, tp_count
    )
    piece = rows // tp_count
    chunks = 2 if piece % 32 == 0 else 1
    residual_mid, ffw_in, *ffw_in_cuts = mid_norm(
        hidden_in, post_attn_gain, pre_ffw_gain, tp_scatter(projected), tp_index, chunks
    )
    own_pieces = tp_gather(ffw_in, tp_count)
    partner_in = [seq_swap(cut, half_count) for cut in ffw_in_cuts]
    partner_pieces = [tp_gather(cut, tp_count) for cut in partner_in]
    pack_one = lambda found, keys, marks: pack_half(
        found, keys, hidden_in.shape[1], gate_up.shape[1], tp_index, seq_index, marks
    )
    if seq_count == 8:
        gates = [
            chain[-1],
            seq_swap(mark, 1),
            own_pieces[:-1],
            partner_pieces,
        ]
        packed = spread_line(low, high, half, gates, pack_one)
    else:
        found = spread_doubling(low, high, half)
        packed = [pack_one(found, range(at, at + half_count), []) for at in (0, half_count)]
    returned = [
        seq_swap(gate_up_act(pieces, [0], 1, packed, half), half_count)
        for pieces in partner_pieces
    ]
    own_act = gate_up_act(own_pieces, list(range(chunks)), chunks, packed, half)
    down_held = hold(down_weight, partner_pieces[0][0])
    next_held = hold(next_weight, own_act)
    result = None
    gathered = []
    for c in range(chunks):
        ffw_out = down(own_act, returned[c], down_held, half, tp_count, c)
        next_in = out_norm(residual_mid, post_ffw_gain, next_gain, tp_scatter(ffw_out), c)
        gathered.append(tp_gather(next_in, tp_count))
    for c in range(chunks):
        result = next_projection(gathered[c], next_held, tp_index, c, chunks, result)
    return result.reshape(rows, next_weight.shape[1])


def solution(mesh):
    in_specs = (
        P("seq", None),
        P("seq", "tp"),
        P(),
        P("tp", None),
        P(None, ("seq", "tp"), None),
        P("tp", None),
        P(None, "tp"),
        P(),
        P(),
        P(),
        P(),
    )
    out_specs = P("seq", "tp")
    return jax.shard_map(local, mesh=mesh, in_specs=in_specs, out_specs=out_specs, check_vma=False)
```

```python
import functools

import jax
import jax.numpy as jnp
from jax import lax
from jax.experimental import pallas as pl
from jax.experimental.pallas import tpu as pltpu
from jax.sharding import PartitionSpec as P

HEADS = 16
KV_HEADS = 8
HEAD_DIM = 256
PER_GROUP = HEADS // KV_HEADS
GROUP_COLS = (PER_GROUP + 2) * HEAD_DIM
MIB = 1 << 20
UNIT = 20_000_000_000
CA = 0.1
CM = 4.0
CC = 1.0
CW = 1.0


def span(units):
    return pl.CostEstimate(flops=int(units * UNIT) + 1, bytes_accessed=1000, transcendentals=0)


COST = span(0)


def rms_norm(values, gain):
    meansq = jnp.mean(values * values, axis=-1, keepdims=True)
    return values * lax.rsqrt(meansq + 1e-06) * gain


def tp_swap(values, bits):
    size = lax.axis_size("tp")
    return lax.ppermute(values, "tp", [(i, i ^ bits) for i in range(size)])


def seq_swap(values, bits):
    size = lax.axis_size("seq")
    return lax.ppermute(values, "seq", [(i, i ^ bits) for i in range(size)])


def seq_up(values):
    size = lax.axis_size("seq")
    return lax.ppermute(values, "seq", [(i, i + 2) for i in range(size - 2)])


def after(values, token):
    return lax.optimization_barrier((values, token))[0]


def hint(values):
    return seq_swap(values[:16, :128], 1)


def attention_kernel(ends_ref, place_ref, joined_ref, o_hbm, *refs, blocks, groups, prompts, parts):
    kv_refs = refs[: blocks * groups]
    out_refs = refs[blocks * groups : blocks * groups + parts]
    mark_ref, peak, total, acc, projected, o_ref, sems = refs[blocks * groups + parts :]
    rows = joined_ref.shape[0]
    piece = rows // parts
    head_cols = PER_GROUP * HEAD_DIM
    fetches = []
    for g in range(groups):
        held = pl.ds(g * head_cols, head_cols)
        fetches.append(pltpu.make_async_copy(o_hbm.at[held], o_ref.at[held], sems.at[g]))
        fetches[-1].start()
    first = place_ref[1]
    stacked = PER_GROUP * rows
    at = first + lax.rem(lax.broadcasted_iota(jnp.int32, (1, stacked), 1), rows)
    start = jnp.zeros_like(at)
    lowest = jnp.int32(0)
    for p in range(prompts):
        end = ends_ref[p]
        start = jnp.where(at >= end, jnp.maximum(start, end), start)
        lowest = jnp.where(first >= end, jnp.maximum(lowest, end), lowest)

    for g in range(groups):
        col = g * GROUP_COLS
        queries = jnp.concatenate(
            [
                joined_ref[:, col + r * HEAD_DIM : col + (r + 1) * HEAD_DIM]
                for r in range(PER_GROUP)
            ],
            axis=0,
        ) * jnp.bfloat16(HEAD_DIM ** (-0.5))

        def scores_of(keys, base, own, queries=queries):
            scores = lax.dot_general(
                keys, queries, (((1,), (1,)), ((), ())), preferred_element_type=jnp.float32
            )
            places = base + lax.broadcasted_iota(jnp.int32, scores.shape, 0)
            kept = (places >= start) & (places <= at) if own else places >= start
            return jnp.where(kept, scores, -1e30)

        def blend(values, weights):
            return lax.dot_general(
                values,
                weights.astype(jnp.bfloat16),
                (((0,), (0,)), ((), ())),
                preferred_element_type=jnp.float32,
            )

        own_keys = joined_ref[:, col + head_cols : col + head_cols + HEAD_DIM]
        own_values = joined_ref[:, col + head_cols + HEAD_DIM : col + GROUP_COLS]
        scores = scores_of(own_keys, first, True)
        top = jnp.max(scores, axis=0, keepdims=True)
        weights = jnp.exp(scores - top)
        peak[...] = top
        total[...] = jnp.sum(weights, axis=0, keepdims=True)
        acc[...] = blend(own_values, weights)
        for i in range(blocks):
            base = place_ref[2 + i]
            kv_ref = kv_refs[i * groups + g]

            @pl.when((base >= 0) & (base + rows > lowest) & (base < first))
            def _(base=base, kv_ref=kv_ref, scores_of=scores_of, blend=blend):
                scores = scores_of(kv_ref[:, :HEAD_DIM], base, False)
                before = peak[...]
                top = jnp.maximum(before, jnp.max(scores, axis=0, keepdims=True))
                weights = jnp.exp(scores - top)
                shrink = jnp.exp(before - top)
                peak[...] = top
                total[...] = total[...] * shrink + jnp.sum(weights, axis=0, keepdims=True)
                acc[...] = acc[...] * shrink + blend(kv_ref[:, HEAD_DIM:], weights)

        result = (acc[...] / total[...]).T.astype(jnp.bfloat16)
        attended = jnp.concatenate(
            [result[r * rows : (r + 1) * rows] for r in range(PER_GROUP)], axis=1
        )
        fetches[g].wait()
        tile = 512
        for j in range(o_ref.shape[1] // tile):
            cut = slice(j * tile, (j + 1) * tile)
            product = jnp.dot(
                attended,
                o_ref[g * head_cols : (g + 1) * head_cols, cut],
                preferred_element_type=jnp.float32,
            )
            if g > 0:
                product = product + projected[:, cut]
            projected[:, cut] = product

    for k in range(parts):
        at_row = pl.multiple_of((place_ref[0] ^ k) * piece, piece)
        out_refs[k][...] = projected[pl.ds(at_row, piece)].astype(jnp.bfloat16)
    mark_ref[...] = projected[:16, :128].astype(jnp.bfloat16)


def attend(joined, o_weight, kv_blocks, bases, ends, tp_index, first, parts):
    rows, cols = joined.shape
    width = o_weight.shape[1]
    groups = cols // GROUP_COLS
    place = jnp.stack([tp_index, first] + bases).astype(jnp.int32)
    count = len(kv_blocks)
    stacked = PER_GROUP * rows
    return pl.pallas_call(
        functools.partial(
            attention_kernel, blocks=count, groups=groups, prompts=ends.shape[0], parts=parts
        ),
        in_specs=[pl.BlockSpec(memory_space=pltpu.SMEM)] * 2
        + [pl.BlockSpec(memory_space=pltpu.VMEM), pl.BlockSpec(memory_space=pl.ANY)]
        + [pl.BlockSpec(memory_space=pltpu.VMEM)] * (count * groups),
        out_specs=[pl.BlockSpec(memory_space=pltpu.VMEM)] * (parts + 1),
        scratch_shapes=[
            pltpu.VMEM((1, stacked), jnp.float32),
            pltpu.VMEM((1, stacked), jnp.float32),
            pltpu.VMEM((HEAD_DIM, stacked), jnp.float32),
            pltpu.VMEM((rows, width), jnp.float32),
            pltpu.VMEM(o_weight.shape, jnp.bfloat16),
            pltpu.SemaphoreType.DMA((groups,)),
        ],
        out_shape=[jax.ShapeDtypeStruct((rows // parts, width), jnp.bfloat16)] * parts
        + [jax.ShapeDtypeStruct((16, 128), jnp.bfloat16)],
        compiler_params=pltpu.CompilerParams(vmem_limit_bytes=48 * MIB),
        cost_estimate=span(CA),
        name="attention",
    )(ends, place, joined, o_weight, *[kv for block in kv_blocks for kv in block])


def mid_norm_kernel(place_ref, hidden_ref, post_ref, pre_ref, *refs, parts):
    residual_ref, out_ref, *chunk_refs = refs[parts:]
    total = refs[0][...].astype(jnp.float32)
    for k in range(1, parts):
        total = total + refs[k][...].astype(jnp.float32)
    residual = hidden_ref[...].astype(jnp.float32) + rms_norm(total, post_ref[...])
    residual_ref[...] = residual
    result = rms_norm(residual, pre_ref[...]).astype(jnp.bfloat16)
    out_ref[...] = result
    for c, ref in enumerate(chunk_refs):
        ref[...] = result[c * ref.shape[0] : (c + 1) * ref.shape[0]]


def mid_norm(hidden, post_gain, pre_gain, partials, tp_index, chunks):
    parts = len(partials)
    shape = partials[0].shape
    cut = (shape[0] // chunks, shape[1])
    whole = pl.BlockSpec(shape, lambda i, *_: (0, 0))
    gain = pl.BlockSpec((1, shape[1]), lambda i, *_: (0, 0))
    return pl.pallas_call(
        functools.partial(mid_norm_kernel, parts=parts),
        grid_spec=pltpu.PrefetchScalarGridSpec(
            num_scalar_prefetch=1,
            grid=(1,),
            in_specs=[pl.BlockSpec(shape, lambda i, place: (place[0], 0)), gain, gain]
            + [whole] * parts,
            out_specs=[whole, whole] + [pl.BlockSpec(cut, lambda i, *_: (0, 0))] * chunks,
        ),
        out_shape=[
            jax.ShapeDtypeStruct(shape, jnp.float32),
            jax.ShapeDtypeStruct(shape, jnp.bfloat16),
        ]
        + [jax.ShapeDtypeStruct(cut, jnp.bfloat16)] * chunks,
        compiler_params=pltpu.CompilerParams(vmem_limit_bytes=32 * MIB),
        cost_estimate=span(CM),
        name="mid_norm",
    )(tp_index[None].astype(jnp.int32), hidden, post_gain[None], pre_gain[None], *partials)


def out_norm_kernel(residual_ref, post_ref, next_ref, *refs, parts):
    total = refs[0][...].astype(jnp.float32)
    for k in range(1, parts):
        total = total + refs[k][...].astype(jnp.float32)
    residual = residual_ref[...] + rms_norm(total, post_ref[...])
    refs[parts][...] = rms_norm(residual, next_ref[...]).astype(jnp.bfloat16)


def out_norm(residual, post_gain, next_gain, partials, chunk):
    parts = len(partials)
    shape = partials[0].shape
    whole = pl.BlockSpec(shape, lambda i: (0, 0))
    gain = pl.BlockSpec((1, shape[1]), lambda i: (0, 0))
    return pl.pallas_call(
        functools.partial(out_norm_kernel, parts=parts),
        grid=(1,),
        in_specs=[pl.BlockSpec(shape, lambda i: (chunk, 0)), gain, gain] + [whole] * parts,
        out_specs=whole,
        out_shape=jax.ShapeDtypeStruct(shape, jnp.bfloat16),
        compiler_params=pltpu.CompilerParams(vmem_limit_bytes=32 * MIB),
        cost_estimate=COST,
        name="out_norm",
    )(residual, post_gain[None], next_gain[None], *partials)


def hold_kernel(mark_ref, src_ref, out_ref, sems):
    rows = src_ref.shape[0] // sems.shape[0]
    copies = [
        pltpu.make_async_copy(
            src_ref.at[pl.ds(i * rows, rows)], out_ref.at[pl.ds(i * rows, rows)], sems.at[i]
        )
        for i in range(sems.shape[0])
    ]
    for copy in copies:
        copy.start()
    for copy in copies:
        copy.wait()


def hold(weight, mark):
    return pl.pallas_call(
        hold_kernel,
        in_specs=[pl.BlockSpec(memory_space=pl.ANY)] * 2,
        out_specs=pl.BlockSpec(memory_space=pltpu.VMEM),
        out_shape=jax.ShapeDtypeStruct(weight.shape, weight.dtype),
        scratch_shapes=[pltpu.SemaphoreType.DMA((4,))],
        compiler_params=pltpu.CompilerParams(vmem_limit_bytes=18 * MIB),
        cost_estimate=COST,
        name="hold",
    )(mark, weight)


def down_kernel(half_ref, own_ref, returned_ref, w_ref, *refs, parts, chunk):
    x_all = refs[parts]
    rows, hidden = returned_ref.shape
    piece = rows // parts
    for half in range(2):

        @pl.when(half_ref[0] == half)
        def _(half=half):
            x_all[:, half * hidden : (half + 1) * hidden] = own_ref[chunk * rows : (chunk + 1) * rows]
            x_all[:, (1 - half) * hidden : (2 - half) * hidden] = returned_ref[...]

    tile = 512

    @pl.loop(0, w_ref.shape[1] // tile)
    def _(j):
        at = pl.ds(pl.multiple_of(j * tile, tile), tile)
        product = jnp.dot(x_all[...], w_ref[:, at], preferred_element_type=jnp.float32)
        for k in range(parts):
            refs[k][:, at] = product[k * piece : (k + 1) * piece].astype(jnp.bfloat16)


def down(own, returned, weight, half, parts, chunk):
    rows, hidden = returned.shape
    width = weight.shape[1]
    return pl.pallas_call(
        functools.partial(down_kernel, parts=parts, chunk=chunk),
        in_specs=[pl.BlockSpec(memory_space=pltpu.SMEM)]
        + [pl.BlockSpec(memory_space=pltpu.VMEM)] * 3,
        out_specs=[pl.BlockSpec(memory_space=pltpu.VMEM)] * parts,
        scratch_shapes=[pltpu.VMEM((rows, 2 * hidden), jnp.bfloat16)],
        out_shape=[jax.ShapeDtypeStruct((rows // parts, width), jnp.bfloat16)] * parts,
        compiler_params=pltpu.CompilerParams(vmem_limit_bytes=24 * MIB),
        cost_estimate=COST,
        name="down",
    )(half[None].astype(jnp.int32), own, returned, weight)


def next_kernel(place_ref, *refs, parts, chunk):
    x_refs, w_ref = refs[:parts], refs[parts]
    out_ref, x_all, held, sems = refs[-4:]
    piece = x_refs[0].shape[0]
    for k in range(parts):
        x_all[k * piece : (k + 1) * piece] = x_refs[k][...]
    tile = 512
    copies = []
    for j in range(w_ref.shape[1] // tile):
        at = pl.ds(j * tile, tile)
        product = jnp.dot(x_all[...], w_ref[:, at], preferred_element_type=jnp.float32)
        for k in range(parts):
            held[j, k] = product[k * piece : (k + 1) * piece].astype(jnp.bfloat16)
            to = out_ref.at[place_ref[0] ^ k, chunk, :, at]
            copies.append(pltpu.make_async_copy(held.at[j, k], to, sems.at[j * parts + k]))
            copies[-1].start()
    for copy in copies:
        copy.wait()


def next_projection(pieces, weight, tp_index, chunk, chunks, before):
    parts = len(pieces)
    piece, width = pieces[0].shape
    cols = weight.shape[1]
    tile = 512
    operands = [tp_index[None].astype(jnp.int32), *pieces, weight]
    specs = [pl.BlockSpec(memory_space=pltpu.SMEM)]
    specs += [pl.BlockSpec(memory_space=pltpu.VMEM)] * (parts + 1)
    aliases = {}
    if before is not None:
        aliases = {len(operands): 0}
        operands.append(before)
        specs.append(pl.BlockSpec(memory_space=pl.ANY))
    return pl.pallas_call(
        functools.partial(next_kernel, parts=parts, chunk=chunk),
        in_specs=specs,
        out_specs=pl.BlockSpec(memory_space=pl.ANY),
        scratch_shapes=[
            pltpu.VMEM((parts * piece, width), jnp.bfloat16),
            pltpu.VMEM((cols // tile, parts, piece, tile), jnp.bfloat16),
            pltpu.SemaphoreType.DMA((cols // tile * parts,)),
        ],
        out_shape=jax.ShapeDtypeStruct((parts, chunks, piece, cols), jnp.bfloat16),
        input_output_aliases=aliases,
        compiler_params=pltpu.CompilerParams(vmem_limit_bytes=24 * MIB),
        cost_estimate=COST,
        name="next_projection",
    )(*operands)


def pack_kernel(place_ref, *refs, buffers, marks):
    w_refs, (out_ref, sems) = refs[:buffers], refs[buffers + marks :]
    copies = []
    for ref in w_refs:
        for k in range(ref.shape[0]):
            to = pl.multiple_of(place_ref[len(copies)], 16)
            copies.append(
                pltpu.make_async_copy(
                    ref.at[k], out_ref.at[pl.ds(to, ref.shape[1])], sems.at[len(copies)]
                )
            )
            copies[-1].start()
    for copy in copies:
        copy.wait()


def pack(buffers, offsets, depth, marks):
    wide = buffers[0].shape[2]
    return pl.pallas_call(
        functools.partial(pack_kernel, buffers=len(buffers), marks=len(marks)),
        in_specs=[pl.BlockSpec(memory_space=pltpu.SMEM)]
        + [pl.BlockSpec(memory_space=pl.ANY)] * (len(buffers) + len(marks)),
        out_specs=pl.BlockSpec(memory_space=pltpu.VMEM),
        out_shape=jax.ShapeDtypeStruct((depth, wide), jnp.bfloat16),
        scratch_shapes=[pltpu.SemaphoreType.DMA((len(offsets),))],
        compiler_params=pltpu.CompilerParams(vmem_limit_bytes=16 * MIB),
        cost_estimate=COST,
        name="pack",
    )(jnp.stack(offsets).astype(jnp.int32), *buffers, *marks)


def gate_up_kernel(half_ref, *refs, parts, picked, chunks):
    x_refs, w_refs = refs[:parts], refs[parts : parts + 2]
    out_ref, x_all, acc = refs[parts + 2 :]
    piece = x_refs[0].shape[0] // chunks
    half_depth, both = w_refs[0].shape
    hidden = both // 2
    for i, chunk in enumerate(picked):
        for k in range(parts):
            at = (i * parts + k) * piece
            x_all[at : at + piece] = x_refs[k][chunk * piece : (chunk + 1) * piece]
    tile = 256 if both % 256 == 0 else 128
    near = pl.multiple_of(half_ref[0] * half_depth, 128)
    far = pl.multiple_of((1 - half_ref[0]) * half_depth, 128)

    @pl.loop(0, both // tile)
    def _(j):
        at = pl.ds(pl.multiple_of(j * tile, tile), tile)
        acc[:, at] = jnp.dot(
            x_all[:, pl.ds(near, half_depth)], w_refs[0][:, at], preferred_element_type=jnp.float32
        ) + jnp.dot(
            x_all[:, pl.ds(far, half_depth)], w_refs[1][:, at], preferred_element_type=jnp.float32
        )

    out_ref[...] = (
        jax.nn.gelu(acc[:, :hidden], approximate=True) * acc[:, hidden:]
    ).astype(jnp.bfloat16)


def gate_up_act(pieces, picked, chunks, packed, half):
    parts = len(pieces)
    piece, depth = pieces[0].shape
    rows = parts * piece * len(picked) // chunks
    wide = packed[0].shape[1]
    return pl.pallas_call(
        functools.partial(gate_up_kernel, parts=parts, picked=picked, chunks=chunks),
        in_specs=[pl.BlockSpec(memory_space=pltpu.SMEM)]
        + [pl.BlockSpec(memory_space=pltpu.VMEM)] * (parts + 2),
        out_specs=pl.BlockSpec(memory_space=pltpu.VMEM),
        out_shape=jax.ShapeDtypeStruct((rows, wide // 2), jnp.bfloat16),
        scratch_shapes=[
            pltpu.VMEM((rows, depth), jnp.bfloat16),
            pltpu.VMEM((rows, wide), jnp.float32),
        ],
        compiler_params=pltpu.CompilerParams(vmem_limit_bytes=28 * MIB),
        cost_estimate=COST,
        name="gate_up",
    )(half[None].astype(jnp.int32), *pieces, *packed)


def gather_weights(gate_up, tp_index, seq_index):
    seq_count, tp_count = lax.axis_size("seq"), lax.axis_size("tp")
    half_count = seq_count // 2
    half = seq_index // half_count
    piece_rows = gate_up.shape[1]
    units = gate_up.shape[2] // tp_count
    hidden = units // 2
    pieces = []
    for k in range(tp_count):
        cut = lax.dynamic_slice(
            gate_up, (0, 0, (tp_index ^ k) * units), (2, piece_rows, units)
        ).astype(jnp.bfloat16)
        pieces.append(tp_swap(cut, k) if k else cut)

    def columns(which):
        cuts = [lax.dynamic_slice_in_dim(p, which * hidden, hidden, 2) for p in pieces]
        cuts = [jnp.concatenate([cut[0], cut[1]], axis=1) for cut in cuts]
        stack = jnp.stack(cuts)
        ordered = [
            lax.dynamic_index_in_dim(stack, tp_index ^ j, 0, keepdims=False)
            for j in range(tp_count)
        ]
        return jnp.concatenate(ordered, axis=0)[None]

    if piece_rows % 16 == 0:
        low, high = assemble(pieces)
    else:
        low, high = columns(0), columns(1)
    return low, high


def spread_doubling(low, high, half):
    half_count = lax.axis_size("seq") // 2
    mine, other = jnp.where(half == 0, low, high), jnp.where(half == 0, high, low)
    found = {0: mine, half_count: seq_swap(other, half_count)}
    bits = 2
    while bits < half_count:
        for key in list(found):
            found[key ^ bits] = seq_swap(found[key], bits)
        bits *= 2
    for key in list(found):
        found[key ^ 1] = seq_swap(found[key], 1)
    return found


def spread_line(low, high, half, gates, pack_one):
    chip = lax.axis_index("seq") // 2
    upper = half == 1

    def up(values, first, count):
        pairs = [(s, s + 2) for s in range(2 * first, 2 * (first + count))]
        return lax.ppermute(values, "seq", pairs)

    def down(values, first, count):
        pairs = [(s + 2, s) for s in range(2 * first, 2 * (first + count))]
        return lax.ppermute(values, "seq", pairs)

    low, high = after((low, high), gates[0])
    mine = jnp.where(upper, high, low)
    up_one, down_one = up(high, 0, 3), down(low, 0, 3)
    handed, seen_one = lax.optimization_barrier(((up_one, down_one), gates[1]))
    up_two = up(jnp.where(chip == 0, low, handed[0]), 0, 3)
    down_two = down(jnp.where(chip == 3, high, handed[1]), 0, 3)
    up_two, down_two = after((up_two, down_two), gates[2])
    up_three, down_three = up(up_two, 2, 1), down(down_two, 0, 1)
    inner = (chip == 1) | (chip == 2)
    found = {
        0: mine,
        2: jnp.where(
            inner, jnp.where(upper, down_two, up_two), jnp.where(upper, up_one, down_one)
        ),
        4: jnp.where(upper, up_two, down_two),
    }
    for key in list(found):
        found[key ^ 1] = seq_swap(found[key], 1)
    near = pack_one(found, range(4), [seen_one])
    (up_three, down_three), (near, found[5], _) = lax.optimization_barrier(
        ((up_three, down_three), (near, found[5], gates[3]))
    )
    found[6] = jnp.where(
        inner, jnp.where(upper, up_one, down_one), jnp.where(upper, up_three, down_three)
    )
    found[7] = [seq_swap(found[6][k : k + 1], 1) for k in range(found[6].shape[0])]
    return [near, pack_one(found, range(4, 8), [])]


def pack_half(found, keys, depth, piece_rows, tp_index, seq_index, marks):
    tp_count, half_count = lax.axis_size("tp"), lax.axis_size("seq") // 2
    buffers, offsets = [], []
    for key in keys:
        base = ((seq_index ^ key) % half_count) * (tp_count * piece_rows)
        parts = found[key] if isinstance(found[key], list) else [found[key]]
        subs = sum(part.shape[0] for part in parts)
        sub_rows = parts[0].shape[1]
        buffers += parts
        for k in range(subs):
            offsets.append(base + (tp_index ^ k) * sub_rows if subs > 1 else base)
    return pack(buffers, offsets, depth // 2, marks)


def assemble_kernel(*refs, parts):
    piece_refs, out_refs = refs[:parts], refs[parts:]
    hidden = piece_refs[0].shape[2] // 2
    for k in range(parts):
        for half in range(2):
            for m in range(2):
                out_refs[half][k, :, m * hidden : (m + 1) * hidden] = piece_refs[k][
                    m, :, half * hidden : (half + 1) * hidden
                ]


def assemble(pieces):
    parts = len(pieces)
    _, rows, units = pieces[0].shape
    return pl.pallas_call(
        functools.partial(assemble_kernel, parts=parts),
        out_shape=[jax.ShapeDtypeStruct((parts, rows, units), jnp.bfloat16)] * 2,
        compiler_params=pltpu.CompilerParams(vmem_limit_bytes=32 * MIB),
        cost_estimate=span(CW),
        name="assemble",
    )(*pieces)


def tp_scatter(partials):
    return [tp_swap(part, k) if k else part for k, part in enumerate(partials)]


def tp_gather(values, parts):
    return [values] + [tp_swap(values, k) for k in range(1, parts)]


def local(
    hidden_in,
    joined_inputs,
    lengths,
    o_weight,
    gate_up,
    down_weight,
    next_weight,
    post_attn_gain,
    pre_ffw_gain,
    post_ffw_gain,
    next_gain,
):
    seq_count, tp_count = lax.axis_size("seq"), lax.axis_size("tp")
    seq_index, tp_index = lax.axis_index("seq"), lax.axis_index("tp")
    rows = hidden_in.shape[0]
    half_count = seq_count // 2
    groups = joined_inputs.shape[1] // GROUP_COLS

    own_kv = [
        joined_inputs[:, g * GROUP_COLS + PER_GROUP * HEAD_DIM : (g + 1) * GROUP_COLS]
        for g in range(groups)
    ]
    chain = [own_kv]
    for _ in range(seq_count // 4):
        chain.append([seq_up(kv) for kv in chain[-1]])
    other = [[seq_swap(kv, 1) for kv in block] for block in chain]
    blocks, bases = [], []
    for j in range(len(chain)):
        if j:
            blocks.append(chain[j])
            bases.append((seq_index - 2 * j) * rows)
        blocks.append(other[j])
        bases.append(((seq_index ^ 1) - 2 * j) * rows)

    half = seq_index // half_count
    low, high = gather_weights(after(gate_up, own_kv[0]), tp_index, seq_index)

    ends = jnp.cumsum(lengths).astype(jnp.int32)
    *projected, mark = attend(
        joined_inputs, o_weight, blocks, bases, ends, tp_index, seq_index * rows, tp_count
    )
    piece = rows // tp_count
    chunks = 2 if piece % 32 == 0 else 1
    residual_mid, ffw_in, *ffw_in_cuts = mid_norm(
        hidden_in, post_attn_gain, pre_ffw_gain, tp_scatter(projected), tp_index, chunks
    )
    own_pieces = tp_gather(ffw_in, tp_count)
    partner_in = [seq_swap(cut, half_count) for cut in ffw_in_cuts]
    partner_pieces = [tp_gather(cut, tp_count) for cut in partner_in]
    pack_one = lambda found, keys, marks: pack_half(
        found, keys, hidden_in.shape[1], gate_up.shape[1], tp_index, seq_index, marks
    )
    if seq_count == 8:
        gates = [
            chain[-1],
            seq_swap(mark, 1),
            own_pieces[:-1],
            partner_pieces,
        ]
        packed = spread_line(low, high, half, gates, pack_one)
    else:
        found = spread_doubling(low, high, half)
        packed = [pack_one(found, range(at, at + half_count), []) for at in (0, half_count)]
    returned = [
        seq_swap(gate_up_act(pieces, [0], 1, packed, half), half_count)
        for pieces in partner_pieces
    ]
    own_act = gate_up_act(own_pieces, list(range(chunks)), chunks, packed, half)
    down_held = hold(down_weight, partner_pieces[0][0])
    next_held = hold(next_weight, own_act)
    result = None
    gathered = []
    for c in range(chunks):
        ffw_out = down(own_act, returned[c], down_held, half, tp_count, c)
        next_in = out_norm(residual_mid, post_ffw_gain, next_gain, tp_scatter(ffw_out), c)
        gathered.append(tp_gather(next_in, tp_count))
    for c in range(chunks):
        result = next_projection(gathered[c], next_held, tp_index, c, chunks, result)
    return result.reshape(rows, next_weight.shape[1])


def solution(mesh):
    in_specs = (
        P("seq", None),
        P("seq", "tp"),
        P(),
        P("tp", None),
        P(None, ("seq", "tp"), None),
        P("tp", None),
        P(None, "tp"),
        P(),
        P(),
        P(),
        P(),
    )
    out_specs = P("seq", "tp")
    return jax.shard_map(local, mesh=mesh, in_specs=in_specs, out_specs=out_specs, check_vma=False)
```

```python
import functools

import jax
import jax.numpy as jnp
from jax import lax
from jax.experimental import pallas as pl
from jax.experimental.pallas import tpu as pltpu
from jax.sharding import PartitionSpec as P

HEADS = 16
KV_HEADS = 8
HEAD_DIM = 256
PER_GROUP = HEADS // KV_HEADS
GROUP_COLS = (PER_GROUP + 2) * HEAD_DIM
MIB = 1 << 20
UNIT = 20_000_000_000
CA = 0.1
CM = 4.0
CC = 1.0
CW = 1.0


def span(units):
    return pl.CostEstimate(flops=int(units * UNIT) + 1, bytes_accessed=1000, transcendentals=0)


COST = span(0)


def rms_norm(values, gain):
    meansq = jnp.mean(values * values, axis=-1, keepdims=True)
    return values * lax.rsqrt(meansq + 1e-06) * gain


def tp_swap(values, bits):
    size = lax.axis_size("tp")
    return lax.ppermute(values, "tp", [(i, i ^ bits) for i in range(size)])


def seq_swap(values, bits):
    size = lax.axis_size("seq")
    return lax.ppermute(values, "seq", [(i, i ^ bits) for i in range(size)])


def seq_up(values):
    size = lax.axis_size("seq")
    return lax.ppermute(values, "seq", [(i, i + 2) for i in range(size - 2)])


def after(values, token):
    return lax.optimization_barrier((values, token))[0]


def hint(values):
    return seq_swap(values[:16, :128], 1)


def attention_kernel(ends_ref, place_ref, joined_ref, o_hbm, *refs, blocks, groups, prompts, parts):
    kv_refs = refs[: blocks * groups]
    out_refs = refs[blocks * groups : blocks * groups + parts]
    mark_ref, peak, total, acc, projected, o_ref, sems = refs[blocks * groups + parts :]
    rows = joined_ref.shape[0]
    piece = rows // parts
    head_cols = PER_GROUP * HEAD_DIM
    fetches = []
    for g in range(groups):
        held = pl.ds(g * head_cols, head_cols)
        fetches.append(pltpu.make_async_copy(o_hbm.at[held], o_ref.at[held], sems.at[g]))
        fetches[-1].start()
    first = place_ref[1]
    stacked = PER_GROUP * rows
    at = first + lax.rem(lax.broadcasted_iota(jnp.int32, (1, stacked), 1), rows)
    start = jnp.zeros_like(at)
    lowest = jnp.int32(0)
    for p in range(prompts):
        end = ends_ref[p]
        start = jnp.where(at >= end, jnp.maximum(start, end), start)
        lowest = jnp.where(first >= end, jnp.maximum(lowest, end), lowest)

    for g in range(groups):
        col = g * GROUP_COLS
        queries = jnp.concatenate(
            [
                joined_ref[:, col + r * HEAD_DIM : col + (r + 1) * HEAD_DIM]
                for r in range(PER_GROUP)
            ],
            axis=0,
        ) * jnp.bfloat16(HEAD_DIM ** (-0.5))

        def scores_of(keys, base, own, queries=queries):
            scores = lax.dot_general(
                keys, queries, (((1,), (1,)), ((), ())), preferred_element_type=jnp.float32
            )
            places = base + lax.broadcasted_iota(jnp.int32, scores.shape, 0)
            kept = (places >= start) & (places <= at) if own else places >= start
            return jnp.where(kept, scores, -1e30)

        def blend(values, weights):
            return lax.dot_general(
                values,
                weights.astype(jnp.bfloat16),
                (((0,), (0,)), ((), ())),
                preferred_element_type=jnp.float32,
            )

        own_keys = joined_ref[:, col + head_cols : col + head_cols + HEAD_DIM]
        own_values = joined_ref[:, col + head_cols + HEAD_DIM : col + GROUP_COLS]
        scores = scores_of(own_keys, first, True)
        top = jnp.max(scores, axis=0, keepdims=True)
        weights = jnp.exp(scores - top)
        peak[...] = top
        total[...] = jnp.sum(weights, axis=0, keepdims=True)
        acc[...] = blend(own_values, weights)
        for i in range(blocks):
            base = place_ref[2 + i]
            kv_ref = kv_refs[i * groups + g]

            @pl.when((base >= 0) & (base + rows > lowest) & (base < first))
            def _(base=base, kv_ref=kv_ref, scores_of=scores_of, blend=blend):
                scores = scores_of(kv_ref[:, :HEAD_DIM], base, False)
                before = peak[...]
                top = jnp.maximum(before, jnp.max(scores, axis=0, keepdims=True))
                weights = jnp.exp(scores - top)
                shrink = jnp.exp(before - top)
                peak[...] = top
                total[...] = total[...] * shrink + jnp.sum(weights, axis=0, keepdims=True)
                acc[...] = acc[...] * shrink + blend(kv_ref[:, HEAD_DIM:], weights)

        result = (acc[...] / total[...]).T.astype(jnp.bfloat16)
        attended = jnp.concatenate(
            [result[r * rows : (r + 1) * rows] for r in range(PER_GROUP)], axis=1
        )
        fetches[g].wait()
        tile = 512
        for j in range(o_ref.shape[1] // tile):
            cut = slice(j * tile, (j + 1) * tile)
            product = jnp.dot(
                attended,
                o_ref[g * head_cols : (g + 1) * head_cols, cut],
                preferred_element_type=jnp.float32,
            )
            if g > 0:
                product = product + projected[:, cut]
            projected[:, cut] = product

    for k in range(parts):
        at_row = pl.multiple_of((place_ref[0] ^ k) * piece, piece)
        out_refs[k][...] = projected[pl.ds(at_row, piece)].astype(jnp.bfloat16)
    mark_ref[...] = projected[:16, :128].astype(jnp.bfloat16)


def attend(joined, o_weight, kv_blocks, bases, ends, tp_index, first, parts):
    rows, cols = joined.shape
    width = o_weight.shape[1]
    groups = cols // GROUP_COLS
    place = jnp.stack([tp_index, first] + bases).astype(jnp.int32)
    count = len(kv_blocks)
    stacked = PER_GROUP * rows
    return pl.pallas_call(
        functools.partial(
            attention_kernel, blocks=count, groups=groups, prompts=ends.shape[0], parts=parts
        ),
        in_specs=[pl.BlockSpec(memory_space=pltpu.SMEM)] * 2
        + [pl.BlockSpec(memory_space=pltpu.VMEM), pl.BlockSpec(memory_space=pl.ANY)]
        + [pl.BlockSpec(memory_space=pltpu.VMEM)] * (count * groups),
        out_specs=[pl.BlockSpec(memory_space=pltpu.VMEM)] * (parts + 1),
        scratch_shapes=[
            pltpu.VMEM((1, stacked), jnp.float32),
            pltpu.VMEM((1, stacked), jnp.float32),
            pltpu.VMEM((HEAD_DIM, stacked), jnp.float32),
            pltpu.VMEM((rows, width), jnp.float32),
            pltpu.VMEM(o_weight.shape, jnp.bfloat16),
            pltpu.SemaphoreType.DMA((groups,)),
        ],
        out_shape=[jax.ShapeDtypeStruct((rows // parts, width), jnp.bfloat16)] * parts
        + [jax.ShapeDtypeStruct((16, 128), jnp.bfloat16)],
        compiler_params=pltpu.CompilerParams(vmem_limit_bytes=48 * MIB),
        cost_estimate=span(CA),
        name="attention",
    )(ends, place, joined, o_weight, *[kv for block in kv_blocks for kv in block])


def mid_norm_kernel(place_ref, hidden_ref, post_ref, pre_ref, *refs, parts):
    residual_ref, out_ref, *chunk_refs = refs[parts:]
    total = refs[0][...].astype(jnp.float32)
    for k in range(1, parts):
        total = total + refs[k][...].astype(jnp.float32)
    residual = hidden_ref[...].astype(jnp.float32) + rms_norm(total, post_ref[...])
    residual_ref[...] = residual
    result = rms_norm(residual, pre_ref[...]).astype(jnp.bfloat16)
    out_ref[...] = result
    for c, ref in enumerate(chunk_refs):
        ref[...] = result[c * ref.shape[0] : (c + 1) * ref.shape[0]]


def mid_norm(hidden, post_gain, pre_gain, partials, tp_index, chunks):
    parts = len(partials)
    shape = partials[0].shape
    cut = (shape[0] // chunks, shape[1])
    whole = pl.BlockSpec(shape, lambda i, *_: (0, 0))
    gain = pl.BlockSpec((1, shape[1]), lambda i, *_: (0, 0))
    return pl.pallas_call(
        functools.partial(mid_norm_kernel, parts=parts),
        grid_spec=pltpu.PrefetchScalarGridSpec(
            num_scalar_prefetch=1,
            grid=(1,),
            in_specs=[pl.BlockSpec(shape, lambda i, place: (place[0], 0)), gain, gain]
            + [whole] * parts,
            out_specs=[whole, whole] + [pl.BlockSpec(cut, lambda i, *_: (0, 0))] * chunks,
        ),
        out_shape=[
            jax.ShapeDtypeStruct(shape, jnp.float32),
            jax.ShapeDtypeStruct(shape, jnp.bfloat16),
        ]
        + [jax.ShapeDtypeStruct(cut, jnp.bfloat16)] * chunks,
        compiler_params=pltpu.CompilerParams(vmem_limit_bytes=32 * MIB),
        cost_estimate=span(CM),
        name="mid_norm",
    )(tp_index[None].astype(jnp.int32), hidden, post_gain[None], pre_gain[None], *partials)


def out_norm_kernel(residual_ref, post_ref, next_ref, *refs, parts):
    total = refs[0][...].astype(jnp.float32)
    for k in range(1, parts):
        total = total + refs[k][...].astype(jnp.float32)
    residual = residual_ref[...] + rms_norm(total, post_ref[...])
    refs[parts][...] = rms_norm(residual, next_ref[...]).astype(jnp.bfloat16)


def out_norm(residual, post_gain, next_gain, partials, chunk):
    parts = len(partials)
    shape = partials[0].shape
    whole = pl.BlockSpec(shape, lambda i: (0, 0))
    gain = pl.BlockSpec((1, shape[1]), lambda i: (0, 0))
    return pl.pallas_call(
        functools.partial(out_norm_kernel, parts=parts),
        grid=(1,),
        in_specs=[pl.BlockSpec(shape, lambda i: (chunk, 0)), gain, gain] + [whole] * parts,
        out_specs=whole,
        out_shape=jax.ShapeDtypeStruct(shape, jnp.bfloat16),
        compiler_params=pltpu.CompilerParams(vmem_limit_bytes=32 * MIB),
        cost_estimate=COST,
        name="out_norm",
    )(residual, post_gain[None], next_gain[None], *partials)


def hold_kernel(mark_ref, src_ref, out_ref, sems):
    rows = src_ref.shape[0] // sems.shape[0]
    copies = [
        pltpu.make_async_copy(
            src_ref.at[pl.ds(i * rows, rows)], out_ref.at[pl.ds(i * rows, rows)], sems.at[i]
        )
        for i in range(sems.shape[0])
    ]
    for copy in copies:
        copy.start()
    for copy in copies:
        copy.wait()


def hold(weight, mark):
    return pl.pallas_call(
        hold_kernel,
        in_specs=[pl.BlockSpec(memory_space=pl.ANY)] * 2,
        out_specs=pl.BlockSpec(memory_space=pltpu.VMEM),
        out_shape=jax.ShapeDtypeStruct(weight.shape, weight.dtype),
        scratch_shapes=[pltpu.SemaphoreType.DMA((4,))],
        compiler_params=pltpu.CompilerParams(vmem_limit_bytes=18 * MIB),
        cost_estimate=COST,
        name="hold",
    )(mark, weight)


def down_kernel(half_ref, own_ref, returned_ref, w_ref, *refs, parts, chunk):
    x_all = refs[parts]
    rows, hidden = returned_ref.shape
    piece = rows // parts
    for half in range(2):

        @pl.when(half_ref[0] == half)
        def _(half=half):
            x_all[:, half * hidden : (half + 1) * hidden] = own_ref[chunk * rows : (chunk + 1) * rows]
            x_all[:, (1 - half) * hidden : (2 - half) * hidden] = returned_ref[...]

    tile = 512

    @pl.loop(0, w_ref.shape[1] // tile)
    def _(j):
        at = pl.ds(pl.multiple_of(j * tile, tile), tile)
        product = jnp.dot(x_all[...], w_ref[:, at], preferred_element_type=jnp.float32)
        for k in range(parts):
            refs[k][:, at] = product[k * piece : (k + 1) * piece].astype(jnp.bfloat16)


def down(own, returned, weight, half, parts, chunk):
    rows, hidden = returned.shape
    width = weight.shape[1]
    return pl.pallas_call(
        functools.partial(down_kernel, parts=parts, chunk=chunk),
        in_specs=[pl.BlockSpec(memory_space=pltpu.SMEM)]
        + [pl.BlockSpec(memory_space=pltpu.VMEM)] * 3,
        out_specs=[pl.BlockSpec(memory_space=pltpu.VMEM)] * parts,
        scratch_shapes=[pltpu.VMEM((rows, 2 * hidden), jnp.bfloat16)],
        out_shape=[jax.ShapeDtypeStruct((rows // parts, width), jnp.bfloat16)] * parts,
        compiler_params=pltpu.CompilerParams(vmem_limit_bytes=24 * MIB),
        cost_estimate=COST,
        name="down",
    )(half[None].astype(jnp.int32), own, returned, weight)


def next_kernel(place_ref, *refs, parts, chunk):
    x_refs, w_ref = refs[:parts], refs[parts]
    out_ref, x_all, held, sems = refs[-4:]
    piece = x_refs[0].shape[0]
    for k in range(parts):
        x_all[k * piece : (k + 1) * piece] = x_refs[k][...]
    tile = 512
    copies = []
    for j in range(w_ref.shape[1] // tile):
        at = pl.ds(j * tile, tile)
        product = jnp.dot(x_all[...], w_ref[:, at], preferred_element_type=jnp.float32)
        for k in range(parts):
            held[j, k] = product[k * piece : (k + 1) * piece].astype(jnp.bfloat16)
            to = out_ref.at[place_ref[0] ^ k, chunk, :, at]
            copies.append(pltpu.make_async_copy(held.at[j, k], to, sems.at[j * parts + k]))
            copies[-1].start()
    for copy in copies:
        copy.wait()


def next_projection(pieces, weight, tp_index, chunk, chunks, before):
    parts = len(pieces)
    piece, width = pieces[0].shape
    cols = weight.shape[1]
    tile = 512
    operands = [tp_index[None].astype(jnp.int32), *pieces, weight]
    specs = [pl.BlockSpec(memory_space=pltpu.SMEM)]
    specs += [pl.BlockSpec(memory_space=pltpu.VMEM)] * (parts + 1)
    aliases = {}
    if before is not None:
        aliases = {len(operands): 0}
        operands.append(before)
        specs.append(pl.BlockSpec(memory_space=pl.ANY))
    return pl.pallas_call(
        functools.partial(next_kernel, parts=parts, chunk=chunk),
        in_specs=specs,
        out_specs=pl.BlockSpec(memory_space=pl.ANY),
        scratch_shapes=[
            pltpu.VMEM((parts * piece, width), jnp.bfloat16),
            pltpu.VMEM((cols // tile, parts, piece, tile), jnp.bfloat16),
            pltpu.SemaphoreType.DMA((cols // tile * parts,)),
        ],
        out_shape=jax.ShapeDtypeStruct((parts, chunks, piece, cols), jnp.bfloat16),
        input_output_aliases=aliases,
        compiler_params=pltpu.CompilerParams(vmem_limit_bytes=24 * MIB),
        cost_estimate=COST,
        name="next_projection",
    )(*operands)


def pack_kernel(place_ref, *refs, buffers, marks):
    w_refs, (out_ref, sems) = refs[:buffers], refs[buffers + marks :]
    copies = []
    for ref in w_refs:
        for k in range(ref.shape[0]):
            to = pl.multiple_of(place_ref[len(copies)], 16)
            copies.append(
                pltpu.make_async_copy(
                    ref.at[k], out_ref.at[pl.ds(to, ref.shape[1])], sems.at[len(copies)]
                )
            )
            copies[-1].start()
    for copy in copies:
        copy.wait()


def pack(buffers, offsets, depth, marks):
    wide = buffers[0].shape[2]
    return pl.pallas_call(
        functools.partial(pack_kernel, buffers=len(buffers), marks=len(marks)),
        in_specs=[pl.BlockSpec(memory_space=pltpu.SMEM)]
        + [pl.BlockSpec(memory_space=pl.ANY)] * (len(buffers) + len(marks)),
        out_specs=pl.BlockSpec(memory_space=pltpu.VMEM),
        out_shape=jax.ShapeDtypeStruct((depth, wide), jnp.bfloat16),
        scratch_shapes=[pltpu.SemaphoreType.DMA((len(offsets),))],
        compiler_params=pltpu.CompilerParams(vmem_limit_bytes=16 * MIB),
        cost_estimate=COST,
        name="pack",
    )(jnp.stack(offsets).astype(jnp.int32), *buffers, *marks)


def gate_up_kernel(half_ref, *refs, parts, picked, chunks):
    x_refs, w_refs = refs[:parts], refs[parts : parts + 2]
    out_ref, x_all, acc = refs[parts + 2 :]
    piece = x_refs[0].shape[0] // chunks
    half_depth, both = w_refs[0].shape
    hidden = both // 2
    for i, chunk in enumerate(picked):
        for k in range(parts):
            at = (i * parts + k) * piece
            x_all[at : at + piece] = x_refs[k][chunk * piece : (chunk + 1) * piece]
    tile = 256 if both % 256 == 0 else 128
    near = pl.multiple_of(half_ref[0] * half_depth, 128)
    far = pl.multiple_of((1 - half_ref[0]) * half_depth, 128)

    @pl.loop(0, both // tile)
    def _(j):
        at = pl.ds(pl.multiple_of(j * tile, tile), tile)
        acc[:, at] = jnp.dot(
            x_all[:, pl.ds(near, half_depth)], w_refs[0][:, at], preferred_element_type=jnp.float32
        ) + jnp.dot(
            x_all[:, pl.ds(far, half_depth)], w_refs[1][:, at], preferred_element_type=jnp.float32
        )

    out_ref[...] = (
        jax.nn.gelu(acc[:, :hidden], approximate=True) * acc[:, hidden:]
    ).astype(jnp.bfloat16)


def gate_up_act(pieces, picked, chunks, packed, half):
    parts = len(pieces)
    piece, depth = pieces[0].shape
    rows = parts * piece * len(picked) // chunks
    wide = packed[0].shape[1]
    return pl.pallas_call(
        functools.partial(gate_up_kernel, parts=parts, picked=picked, chunks=chunks),
        in_specs=[pl.BlockSpec(memory_space=pltpu.SMEM)]
        + [pl.BlockSpec(memory_space=pltpu.VMEM)] * (parts + 2),
        out_specs=pl.BlockSpec(memory_space=pltpu.VMEM),
        out_shape=jax.ShapeDtypeStruct((rows, wide // 2), jnp.bfloat16),
        scratch_shapes=[
            pltpu.VMEM((rows, depth), jnp.bfloat16),
            pltpu.VMEM((rows, wide), jnp.float32),
        ],
        compiler_params=pltpu.CompilerParams(vmem_limit_bytes=28 * MIB),
        cost_estimate=COST,
        name="gate_up",
    )(half[None].astype(jnp.int32), *pieces, *packed)


def gather_weights(gate_up, tp_index, seq_index):
    seq_count, tp_count = lax.axis_size("seq"), lax.axis_size("tp")
    half_count = seq_count // 2
    half = seq_index // half_count
    piece_rows = gate_up.shape[1]
    units = gate_up.shape[2] // tp_count
    hidden = units // 2
    pieces = []
    for k in range(tp_count):
        cut = lax.dynamic_slice(
            gate_up, (0, 0, (tp_index ^ k) * units), (2, piece_rows, units)
        ).astype(jnp.bfloat16)
        pieces.append(tp_swap(cut, k) if k else cut)

    def columns(which):
        cuts = [lax.dynamic_slice_in_dim(p, which * hidden, hidden, 2) for p in pieces]
        cuts = [jnp.concatenate([cut[0], cut[1]], axis=1) for cut in cuts]
        stack = jnp.stack(cuts)
        ordered = [
            lax.dynamic_index_in_dim(stack, tp_index ^ j, 0, keepdims=False)
            for j in range(tp_count)
        ]
        return jnp.concatenate(ordered, axis=0)[None]

    if piece_rows % 16 == 0:
        low, high = assemble(pieces)
    else:
        low, high = columns(0), columns(1)
    return low, high


def spread_doubling(low, high, half):
    half_count = lax.axis_size("seq") // 2
    mine, other = jnp.where(half == 0, low, high), jnp.where(half == 0, high, low)
    found = {0: mine, half_count: seq_swap(other, half_count)}
    bits = 2
    while bits < half_count:
        for key in list(found):
            found[key ^ bits] = seq_swap(found[key], bits)
        bits *= 2
    for key in list(found):
        found[key ^ 1] = seq_swap(found[key], 1)
    return found


def spread_line(low, high, half, gates, pack_one):
    chip = lax.axis_index("seq") // 2
    upper = half == 1

    def up(values, first, count):
        pairs = [(s, s + 2) for s in range(2 * first, 2 * (first + count))]
        return lax.ppermute(values, "seq", pairs)

    def down(values, first, count):
        pairs = [(s + 2, s) for s in range(2 * first, 2 * (first + count))]
        return lax.ppermute(values, "seq", pairs)

    low, high = after((low, high), gates[0])
    mine = jnp.where(upper, high, low)
    up_one, down_one = up(high, 0, 3), down(low, 0, 3)
    handed, seen_one = lax.optimization_barrier(((up_one, down_one), gates[1]))
    up_two = up(jnp.where(chip == 0, low, handed[0]), 0, 3)
    down_two = down(jnp.where(chip == 3, high, handed[1]), 0, 3)
    up_two, down_two = after((up_two, down_two), gates[2])
    up_three, down_three = up(up_two, 2, 1), down(down_two, 0, 1)
    inner = (chip == 1) | (chip == 2)
    found = {
        0: mine,
        2: jnp.where(
            inner, jnp.where(upper, down_two, up_two), jnp.where(upper, up_one, down_one)
        ),
        4: jnp.where(upper, up_two, down_two),
    }
    for key in list(found):
        found[key ^ 1] = seq_swap(found[key], 1)
    near = pack_one(found, range(4), [seen_one])
    (up_three, down_three), (near, found[5], _) = lax.optimization_barrier(
        ((up_three, down_three), (near, found[5], gates[3]))
    )
    found[6] = jnp.where(
        inner, jnp.where(upper, up_one, down_one), jnp.where(upper, up_three, down_three)
    )
    found[7] = [seq_swap(found[6][k : k + 1], 1) for k in range(found[6].shape[0])]
    return [near, pack_one(found, range(4, 8), [])]


def pack_half(found, keys, depth, piece_rows, tp_index, seq_index, marks):
    tp_count, half_count = lax.axis_size("tp"), lax.axis_size("seq") // 2
    buffers, offsets = [], []
    for key in keys:
        base = ((seq_index ^ key) % half_count) * (tp_count * piece_rows)
        parts = found[key] if isinstance(found[key], list) else [found[key]]
        subs = sum(part.shape[0] for part in parts)
        sub_rows = parts[0].shape[1]
        buffers += parts
        for k in range(subs):
            offsets.append(base + (tp_index ^ k) * sub_rows if subs > 1 else base)
    return pack(buffers, offsets, depth // 2, marks)


def assemble_kernel(*refs, parts):
    piece_refs, out_refs = refs[:parts], refs[parts:]
    hidden = piece_refs[0].shape[2] // 2
    for k in range(parts):
        for half in range(2):
            for m in range(2):
                out_refs[half][k, :, m * hidden : (m + 1) * hidden] = piece_refs[k][
                    m, :, half * hidden : (half + 1) * hidden
                ]


def assemble(pieces):
    parts = len(pieces)
    _, rows, units = pieces[0].shape
    return pl.pallas_call(
        functools.partial(assemble_kernel, parts=parts),
        out_shape=[jax.ShapeDtypeStruct((parts, rows, units), jnp.bfloat16)] * 2,
        compiler_params=pltpu.CompilerParams(vmem_limit_bytes=32 * MIB),
        cost_estimate=span(CW),
        name="assemble",
    )(*pieces)


def tp_scatter(partials):
    return [tp_swap(part, k) if k else part for k, part in enumerate(partials)]


def tp_gather(values, parts):
    return [values] + [tp_swap(values, k) for k in range(1, parts)]


def local(
    hidden_in,
    joined_inputs,
    lengths,
    o_weight,
    gate_up,
    down_weight,
    next_weight,
    post_attn_gain,
    pre_ffw_gain,
    post_ffw_gain,
    next_gain,
):
    seq_count, tp_count = lax.axis_size("seq"), lax.axis_size("tp")
    seq_index, tp_index = lax.axis_index("seq"), lax.axis_index("tp")
    rows = hidden_in.shape[0]
    half_count = seq_count // 2
    groups = joined_inputs.shape[1] // GROUP_COLS

    own_kv = [
        joined_inputs[:, g * GROUP_COLS + PER_GROUP * HEAD_DIM : (g + 1) * GROUP_COLS]
        for g in range(groups)
    ]
    chain = [own_kv]
    for _ in range(seq_count // 4):
        chain.append([seq_up(kv) for kv in chain[-1]])
    other = [[seq_swap(kv, 1) for kv in block] for block in chain]
    blocks, bases = [], []
    for j in range(len(chain)):
        if j:
            blocks.append(chain[j])
            bases.append((seq_index - 2 * j) * rows)
        blocks.append(other[j])
        bases.append(((seq_index ^ 1) - 2 * j) * rows)

    half = seq_index // half_count
    low, high = gather_weights(after(gate_up, own_kv[0]), tp_index, seq_index)

    ends = jnp.cumsum(lengths).astype(jnp.int32)
    *projected, mark = attend(
        joined_inputs, o_weight, blocks, bases, ends, tp_index, seq_index * rows, tp_count
    )
    piece = rows // tp_count
    chunks = 2 if piece % 32 == 0 else 1
    residual_mid, ffw_in, *ffw_in_cuts = mid_norm(
        hidden_in, post_attn_gain, pre_ffw_gain, tp_scatter(projected), tp_index, chunks
    )
    own_pieces = tp_gather(ffw_in, tp_count)
    partner_in = [seq_swap(cut, half_count) for cut in ffw_in_cuts]
    partner_pieces = [tp_gather(cut, tp_count) for cut in partner_in]
    pack_one = lambda found, keys, marks: pack_half(
        found, keys, hidden_in.shape[1], gate_up.shape[1], tp_index, seq_index, marks
    )
    if seq_count == 8:
        gates = [
            chain[-1],
            seq_swap(mark, 1),
            own_pieces[:-1],
            partner_pieces,
        ]
        packed = spread_line(low, high, half, gates, pack_one)
    else:
        found = spread_doubling(low, high, half)
        packed = [pack_one(found, range(at, at + half_count), []) for at in (0, half_count)]
    returned = [
        seq_swap(gate_up_act(pieces, [0], 1, packed, half), half_count)
        for pieces in partner_pieces
    ]
    own_act = [gate_up_act(own_pieces, [c], chunks, packed, half) for c in range(chunks)]
    down_held = hold(down_weight, partner_pieces[0][0])
    next_held = hold(next_weight, own_act[0])
    result = None
    gathered = []
    for c in range(chunks):
        ffw_out = down(own_act[c], returned[c], down_held, half, tp_count, 0)
        next_in = out_norm(residual_mid, post_ffw_gain, next_gain, tp_scatter(ffw_out), c)
        gathered.append(tp_gather(next_in, tp_count))
    for c in range(chunks):
        result = next_projection(gathered[c], next_held, tp_index, c, chunks, result)
    return result.reshape(rows, next_weight.shape[1])


def solution(mesh):
    in_specs = (
        P("seq", None),
        P("seq", "tp"),
        P(),
        P("tp", None),
        P(None, ("seq", "tp"), None),
        P("tp", None),
        P(None, "tp"),
        P(),
        P(),
        P(),
        P(),
    )
    out_specs = P("seq", "tp")
    return jax.shard_map(local, mesh=mesh, in_specs=in_specs, out_specs=out_specs, check_vma=False)
```
